512 devices in a mesh: slab: 16 (over x_lo, y, core), coef: 32 (over x_hi, z).
Axes of the slice: x: 4 (x_hi: 2, x_lo: 2; x = x_hi * 2 + x_lo), y: 4, z: 16, core: 2. Of those that a mesh axis runs over, the one named last changes fastest.
Arguments:
- cotangent: float32 [8192, 4096], P('slab', 'coef'), may hold values from -6 to 6
- transport_state: bfloat16 [8192, 4096], P('slab', 'coef'), may hold values from -6 to 6
- source_state: bfloat16 [8192, 4096], P('slab', 'coef'), may hold values from -6 to 6
- courant: float32 [8192], P('slab'), may hold values from 0.2 to 1.2
- upwind_codes: int32 [8192], P('slab'), may hold values from 0 to 1
- strain_rate: float32 [9, 8192], P(None, ('slab', 'coef')), may hold values from -4 to 4
Outputs:
- adj_source: float32 [8192, 4096], P('slab', 'coef')
- adj_strain: float32 [9, 8192], P(None, ('slab', 'coef'))
- adj_courant: float32 [8192], P(('slab', 'coef'))
The draws below stay inside these ranges and needn't reach their ends.
All inputs are finite; a program needn't handle non-finite values.
Results may differ from the reference program's by a relative error of at most 0.0003.
Values may be sent and summed in bfloat16 or wider, within the bound.
A program may use at most 64 MiB of HBM per device.

```python
import math
import jax
import jax.numpy as jnp
from jax import lax

CYZ = 128
NH = 16
QP = 24
K = 4096
CELLS = 8192


def place_ends(values, key, low, top_value):
    extent = values.shape
    place = [jax.random.randint(jax.random.fold_in(key, axis), (), 0, extent[axis]) for axis in range(len(extent))]
    values = values.at[tuple(place)].set(low)
    longest = extent.index(max(extent))
    place[longest] = (place[longest] + 1) % extent[longest]
    return values.at[tuple(place)].set(top_value)


def spiked(result, stream_key, source, target, shards_of, factor):
    def block_of(dim):
        return (jnp.arange(result.shape[dim]) // (result.shape[dim] // shards_of)).reshape((-1,) + (1,) * (result.ndim - 1 - dim))

    one_side = jax.random.permutation(stream_key, shards_of)[block_of(target)]
    second = (block_of(target) + shards_of // 2) % shards_of
    return jnp.where((block_of(source) == one_side) | (block_of(source) == second), factor * result, result)


def levels(key, shape, shards, least, top_value):
    level = 1.0
    for position, shards_of in shards:
        steps = jax.random.uniform(jax.random.fold_in(jax.random.fold_in(key, 6), position), (shards_of,), jnp.float32, least / len(shards), top_value / len(shards))
        level = level * jnp.repeat(jnp.exp(steps), shape[position] // shards_of).reshape((-1,) + (1,) * (len(shape) - 1 - position))
    return level


def noise(stream_key, extent, width, limit, split=(), kind=jnp.bfloat16):
    result = width * jax.random.normal(stream_key, extent, jnp.float32)
    if split:
        result = result * levels(stream_key, extent, split, -0.22, 0.18)
    return jnp.clip(result, -limit, limit).astype(kind)


def heavy_noise(stream_key, shape, scale, reach, shards, heavy, held_as=jnp.bfloat16):
    result = scale * jax.random.normal(stream_key, shape, jnp.float32)
    if shards:
        result = result * levels(stream_key, shape, shards, -0.22, 0.18)
    return jnp.clip(spiked(result, jax.random.fold_in(stream_key, 3), *heavy), -reach, reach).astype(held_as)


def setup_inputs(seed: int = 0) -> dict:
    keys = jax.random.split(jax.random.key(seed), 7)
    cotangent = heavy_noise(keys[0], (CELLS, K), 1.0, 6.0, ((0, 16), (1, 32)), (1, 0, 32, 2.75), jnp.float32)
    transport_state = noise(keys[1], (CELLS, K), 1.0, 6.0, ((0, 16), (1, 32)))
    source_state = heavy_noise(keys[2], (CELLS, K), 1.0, 6.0, ((0, 16), (1, 32)), (1, 0, 32, 2.75))
    courant = jnp.clip(0.2 + 1 * jax.random.uniform(keys[3], (CELLS,), jnp.float32) ** levels(keys[3], (CELLS,), ((0, 16),), -0.2, 0.2), 0.2, 1.2)
    upwind_codes = place_ends(jax.random.randint(keys[4], (CELLS,), 0, 2), jax.random.fold_in(keys[4], 1), 0, 1).astype(jnp.int32)
    strain_rate = noise(keys[5], (9, CELLS), 1.0, 4.0, ((1, 512),), jnp.float32)
    return dict(cotangent=cotangent, transport_state=transport_state, source_state=source_state, courant=courant, upwind_codes=upwind_codes, strain_rate=strain_rate)


section_weights = (0.25, 1.0 / 3.0, 0.5, 1.0)
quad_half = 4.5
fene_limit = 64.0
time_step = 0.005
highest = lax.Precision.HIGHEST

def hermite_table(mode_count, points):
    node_list = quad_half * (2.0 * jnp.arange(points, dtype=jnp.float32) + 1.0 - points) / points
    leading = jnp.exp(-0.5 * node_list * node_list) * math.pi ** (-0.25)
    table_rows = [leading, math.sqrt(2.0) * node_list * leading]
    for degree in range(1, mode_count - 1):
        table_rows.append(math.sqrt(2.0 / (degree + 1.0)) * node_list * table_rows[degree] - math.sqrt(degree / (degree + 1.0)) * table_rows[degree - 1])
    return (jnp.stack(table_rows[:mode_count]), node_list)

def quadrature_tables(mode_count, points):
    hermite, node_list = hermite_table(mode_count, points)
    cube_shape = (points, points, points)
    coords = (jnp.broadcast_to(node_list[:, None, None], cube_shape).reshape(-1), jnp.broadcast_to(node_list[None, :, None], cube_shape).reshape(-1), jnp.broadcast_to(node_list[None, None, :], cube_shape).reshape(-1))
    spring = 1.0 - (coords[0] * coords[0] + coords[1] * coords[1] + coords[2] * coords[2]) / fene_limit
    pair_table = jnp.stack([coords[left_dim] * coords[right_dim] / spring for left_dim in range(3) for right_dim in range(3)])
    return (hermite, pair_table)

def to_values(coeffs, hermite):
    step_one = jnp.einsum('cijk,kd->cijd', coeffs, hermite, precision=highest)
    step_two = jnp.einsum('cijd,jb->cibd', step_one, hermite, precision=highest)
    return jnp.einsum('cibd,ia->cabd', step_two, hermite, precision=highest)

def to_coefs(values, hermite):
    step_one = jnp.einsum('cabd,ia->cibd', values, hermite, precision=highest)
    step_two = jnp.einsum('cibd,jb->cijd', step_one, hermite, precision=highest)
    return jnp.einsum('cijd,kd->cijk', step_two, hermite, precision=highest)

def reference(cotangent, transport_state, source_state, courant, upwind_codes, strain_rate):
    plane_total = CELLS // CYZ
    speed_grid = courant.reshape(plane_total, CYZ, 1)
    upper_mask = (upwind_codes == 1).astype(jnp.float32).reshape(plane_total, CYZ, 1)
    lower_mask = 1.0 - upper_mask
    coef_block = math.gcd(K, 128)
    block_total = K // coef_block

    def difference(field):
        below = jnp.roll(field, 1, axis=0)
        above = jnp.roll(field, -1, axis=0)
        return lower_mask * (field - below) + upper_mask * (above - field)

    def spread_back(weighted):
        low_part = lower_mask * weighted
        high_part = upper_mask * weighted
        return low_part - jnp.roll(low_part, -1, axis=0) - high_part + jnp.roll(high_part, 1, axis=0)

    def transport_block(block_no):
        start_col = (block_no * coef_block).astype(jnp.int32)
        cot_part = lax.dynamic_slice_in_dim(cotangent, start_col, coef_block, 1)
        initial = lax.dynamic_slice_in_dim(transport_state, start_col, coef_block, 1).astype(jnp.float32)
        initial = initial.reshape(plane_total, CYZ, coef_block)
        differences = []
        section_now = initial
        for section_no in range(4):
            change = difference(section_now)
            differences.append(change)
            section_now = initial - section_weights[section_no] * speed_grid * change
        adjoint = cot_part.reshape(plane_total, CYZ, coef_block)
        accumulated = jnp.zeros((plane_total, CYZ, coef_block), jnp.float32)
        speed_part = jnp.zeros((plane_total, CYZ), jnp.float32)
        for section_no in (3, 2, 1, 0):
            speed_part = speed_part - section_weights[section_no] * lax.optimization_barrier(jnp.sum(adjoint * differences[section_no], axis=2))
            accumulated = accumulated + adjoint
            adjoint = -section_weights[section_no] * spread_back(speed_grid * adjoint)
        return (accumulated + adjoint, speed_part)
    mu_blocks, speed_blocks = lax.map(transport_block, jnp.arange(block_total, dtype=jnp.int32))
    mu_field = jnp.transpose(mu_blocks, (1, 2, 0, 3)).reshape(CELLS, K)
    adj_courant = lax.optimization_barrier(jnp.sum(speed_blocks, axis=0)).reshape(CELLS) / math.sqrt(K)
    hermite, pair_table = quadrature_tables(NH, QP)
    cell_block = math.gcd(CELLS, 512)
    cell_groups = CELLS // cell_block
    weight_cube = (2.0 * quad_half / QP) ** 3

    def config_block(operands):
        mu_part, source_part, strain_part = operands
        adj_values = weight_cube * to_values(mu_part.reshape(cell_block, NH, NH, NH), hermite).reshape(cell_block, QP ** 3)
        source_values = to_values(source_part.astype(jnp.float32).reshape(cell_block, NH, NH, NH), hermite)
        source_values = source_values.reshape(cell_block, QP ** 3)
        multiplier = 1.0 + time_step * jnp.dot(strain_part, pair_table, preferred_element_type=jnp.float32, precision=highest)
        adj_part = to_coefs((multiplier * adj_values).reshape(cell_block, QP, QP, QP), hermite).reshape(cell_block, K)
        strain_grad = time_step * jnp.dot(adj_values * source_values, pair_table.T, preferred_element_type=jnp.float32, precision=highest)
        return (adj_part, strain_grad)
    adj_groups, strain_groups = lax.map(config_block, (mu_field.reshape(cell_groups, cell_block, K), source_state.reshape(cell_groups, cell_block, K), strain_rate.T.reshape(cell_groups, cell_block, 9)))
    return (adj_groups.reshape(CELLS, K), strain_groups.reshape(CELLS, 9).T, adj_courant)
```

```python
import functools
import math

import jax
import jax.numpy as jnp
import ml_dtypes
import numpy as np
from jax import lax
from jax.experimental import pallas as pl
from jax.experimental.pallas import tpu as pltpu
from jax.sharding import PartitionSpec as P

CYZ = 128
NH = 16
QP = 24
K = 4096
PLANES = 4
SLABS = 16
OWNERS = 32
CELLS = 16
WIDTH = 128
POINTS = QP * QP

section_weights = (0.25, 1.0 / 3.0, 0.5, 1.0)
quad_half = 4.5
fene_limit = 64.0
time_step = 0.005
weight_cube = (2.0 * quad_half / QP) ** 3
code_top = 32600.0
f32 = jnp.float32
bf16 = jnp.bfloat16
MESH = pl.DeviceIdType.MESH


def split_table(table):
    high = table.astype(np.float32).astype(ml_dtypes.bfloat16)
    low = (table - high.astype(np.float64)).astype(np.float32).astype(ml_dtypes.bfloat16)
    return np.stack([high, low])


@functools.cache
def tables():
    x = quad_half * (2.0 * np.arange(QP) + 1.0 - QP) / QP
    rows = [np.exp(-0.5 * x * x) * math.pi ** (-0.25)]
    rows.append(math.sqrt(2.0) * x * rows[0])
    for m in range(1, NH - 1):
        rows.append(
            math.sqrt(2.0 / (m + 1.0)) * x * rows[m] - math.sqrt(m / (m + 1.0)) * rows[m - 1]
        )
    h = np.stack(rows)
    inner = np.kron(h, h)
    outer = np.kron(h.T, np.eye(CELLS))
    xb = np.repeat(x, QP)
    xd = np.tile(x, QP)
    square = x[:, None] ** 2 + (xb**2 + xd**2)[None, :]
    ratio = time_step / (1.0 - square / fene_limit)
    zero = np.zeros(POINTS)
    one = np.ones(POINTS)
    moments = np.zeros((3, 16, POINTS))
    moments[0, [4, 5, 7, 8]] = [xb * xb, xb * xd, xb * xd, xd * xd]
    moments[1, [1, 2, 3, 6]] = [xb, xd, xb, xd]
    moments[2, 0] = one
    points = np.stack([xb, xd, xb * xb, xb * xd, xd * xd, zero, zero, zero])
    return (
        x,
        split_table(outer),
        split_table(inner),
        split_table(np.ascontiguousarray(inner.T)),
        split_table(np.ascontiguousarray(outer.T)),
        ratio.astype(np.float32),
        points.astype(np.float32),
        moments.astype(np.float32),
    )


def halves(value):
    high = value.astype(bf16)
    return high, (value - high.astype(f32)).astype(bf16)


def product(left, right):
    total = None
    for i, a in enumerate(left):
        for j, b in enumerate(right):
            if i + j < 2:
                part = jnp.dot(a, b, preferred_element_type=f32)
                total = part if total is None else total + part
    return total


def encode(low, high):
    top = jnp.max(jnp.maximum(jnp.abs(low), jnp.abs(high)), axis=0, keepdims=True)
    level = jnp.ceil(jnp.log2(jnp.maximum(top, 1e-30)) * 8.0)
    unit = jnp.exp2(level * -0.125) * code_top
    low_code = jnp.round(low * unit).astype(jnp.int32)
    high_code = jnp.round(high * unit).astype(jnp.int32)
    word = jnp.bitwise_or(lax.shift_left(high_code, 16), jnp.bitwise_and(low_code, 0xFFFF))
    return word, level.astype(jnp.int32)


def decode(word, level, factor):
    unit = jnp.exp2(level.astype(f32) * 0.125) * (factor / code_top)
    low = lax.shift_right_arithmetic(lax.shift_left(word, 16), 16).astype(f32) * unit
    high = lax.shift_right_arithmetic(word, 16).astype(f32) * unit
    return low, high


def kernel(
    nodes,
    cot, tst, src, cou, cod, strain,
    outer_hbm, inner_hbm, inner_t_hbm, outer_t_hbm, ratio_ref, points_ref, moments_ref,
    out_source, out_strain, out_courant,
    gbuf, tbuf, scbuf, sct_buf, acc_buf,
    src_recv, mu_send, mu_recv, back_send, back_recv, speed_send, speed_recv,
    outer_ref, inner_ref, inner_t_ref, outer_t_ref,
    u_buf, es_buf, square_buf, line_buf, column_buf,
    local_sem, halo_send, halo_recv, all_send, all_recv,
):
    me = lax.axis_index("coef")
    slab = lax.axis_index("slab")
    above = lax.rem(slab + 1, SLABS)
    below = lax.rem(slab + SLABS - 1, SLABS)
    rows = PLANES * CYZ

    loads = [
        pltpu.make_async_copy(cot, gbuf.at[pl.ds(rows, rows)], local_sem.at[0]),
        pltpu.make_async_copy(tst, tbuf.at[pl.ds(rows, rows)], local_sem.at[1]),
        pltpu.make_async_copy(outer_hbm, outer_ref, local_sem.at[2]),
        pltpu.make_async_copy(inner_hbm, inner_ref, local_sem.at[3]),
        pltpu.make_async_copy(inner_t_hbm, inner_t_ref, local_sem.at[4]),
        pltpu.make_async_copy(outer_t_hbm, outer_t_ref, local_sem.at[5]),
        pltpu.make_async_copy(
            src.at[pl.ds(pl.multiple_of(me * CELLS, CELLS), CELLS)],
            src_recv.at[lax.rem(me, 2), lax.div(me, 2)],
            local_sem.at[6],
        ),
    ]
    barrier = pltpu.get_barrier_semaphore()

    def greet(off, _):
        pl.semaphore_signal(
            barrier, inc=1, device_id={"coef": lax.rem(me + off, OWNERS)}, device_id_type=MESH
        )
        return 0

    pl.semaphore_signal(barrier, inc=1, device_id={"slab": above}, device_id_type=MESH)
    pl.semaphore_signal(barrier, inc=1, device_id={"slab": below}, device_id_type=MESH)
    lax.fori_loop(1, OWNERS, greet, 0)
    for load in loads:
        load.start()
    scbuf[1] = jnp.where(cod[...] == 1, -cou[...], cou[...])
    pl.semaphore_wait(barrier, OWNERS + 1)

    halos = []
    for way, target, place in ((0, above, 0), (1, below, 2)):
        here = pl.ds(place * rows, rows)
        for kind, source, dest in (
            (0, scbuf.at[1], scbuf.at[place]),
            (1, tst, tbuf.at[here]),
            (2, cot, gbuf.at[here]),
        ):
            halos.append(
                pltpu.make_async_remote_copy(
                    src_ref=source,
                    dst_ref=dest,
                    send_sem=halo_send.at[way, kind],
                    recv_sem=halo_recv.at[way, kind],
                    device_id={"slab": target},
                    device_id_type=MESH,
                )
            )
    for halo in halos:
        halo.start()

    my_half, my_mode = lax.rem(me, 2), lax.div(me, 2)

    def send_source(off, _):
        dest = lax.rem(me + off, OWNERS)
        pltpu.make_async_remote_copy(
            src_ref=src.at[pl.ds(pl.multiple_of(dest * CELLS, CELLS), CELLS)],
            dst_ref=src_recv.at[my_half, my_mode],
            send_sem=all_send.at[0],
            recv_sem=all_recv.at[0],
            device_id={"coef": dest},
            device_id_type=MESH,
        ).start()
        return 0

    lax.fori_loop(1, OWNERS, send_source, 0)

    column_buf[...] = jnp.zeros((128, 128), f32)
    column_buf[0:9, 0:16] = strain[...]
    turned = jnp.transpose(column_buf[...])[0:16]
    col = [turned[:, p : p + 1] for p in range(9)]
    pts = [points_ref[n : n + 1] for n in range(5)]
    line_buf[...] = (col[1] + col[3]) * pts[0] + (col[2] + col[6]) * pts[1]
    square_buf[...] = col[4] * pts[2] + (col[5] + col[7]) * pts[3] + col[8] * pts[4]

    loads[0].wait()
    loads[1].wait()
    for halo in halos:
        halo.wait()
    signed = jnp.concatenate([scbuf[0], scbuf[1], scbuf[2], jnp.zeros((116, 128), f32)], axis=0)
    sct_buf[...] = jnp.transpose(signed)

    def chunk(step, _):
        part = lax.rem(me + step, 8)
        mu_parts = []
        for h in range(2):
            y = pl.multiple_of(part * 16 + h * 8, 8)
            sct = sct_buf[pl.ds(y, 8), :]
            wide = [jnp.broadcast_to(sct[:, p : p + 1], (8, WIDTH)) for p in range(12)]
            upper = [c < 0.0 for c in wide]
            c0 = [jnp.maximum(c, 0.0) for c in wide]
            c1 = [jnp.maximum(-c, 0.0) for c in wide]
            speed = [jnp.abs(c) for c in wide]
            s0 = [
                tbuf[pl.ds(pl.multiple_of(p * CYZ + part * 16, 16), 16), :].astype(f32)[
                    h * 8 : h * 8 + 8
                ]
                for p in range(12)
            ]
            s = dict(enumerate(s0))
            own = []
            for n in range(4):
                edge = {p: s[p + 1] - s[p] for p in range(n, 11 - n)}
                change = {p: jnp.where(upper[p], edge[p], edge[p - 1]) for p in range(n + 1, 11 - n)}
                own.append([change[p] for p in range(4, 8)])
                if n < 3:
                    s = {p: s0[p] - section_weights[n] * speed[p] * change[p] for p in change}
            g = {p: gbuf[pl.ds(p * CYZ + y, 8), :] for p in range(12)}
            mu = [g[p] for p in range(4, 8)]
            acc = [None] * 4
            for k, n in enumerate((3, 2, 1, 0)):
                for p in range(4):
                    term = section_weights[n] * (g[p + 4] * own[n][p])
                    acc[p] = term if acc[p] is None else acc[p] + term
                flow = {p: c1[p] * g[p] + c0[p + 1] * g[p + 1] for p in range(k, 11 - k)}
                g = {p: section_weights[n] * (flow[p] - flow[p - 1]) for p in range(k + 1, 11 - k)}
                mu = [mu[p] + g[p + 4] for p in range(4)]
            for p in range(4):
                acc_buf[p, pl.ds(y, 8), :] = acc[p]
            mu_parts.append(mu)
        for p in range(4):
            dest = p * 8 + part
            word, level = encode(mu_parts[0][p], mu_parts[1][p])
            mu_send[dest, 0:8, :] = word
            mu_send[dest, 8:9, :] = level
            where_to = mu_recv.at[my_half, my_mode]

            @pl.when(dest != me)
            def _():
                pltpu.make_async_remote_copy(
                    src_ref=mu_send.at[dest],
                    dst_ref=where_to,
                    send_sem=all_send.at[1],
                    recv_sem=all_recv.at[1],
                    device_id={"coef": dest},
                    device_id_type=MESH,
                ).start()

            @pl.when(dest == me)
            def _():
                pltpu.make_async_copy(mu_send.at[dest], where_to, local_sem.at[7]).start()

        return 0

    lax.fori_loop(0, 8, chunk, 0)

    ones = jnp.ones((8, WIDTH), bf16)
    for p in range(4):
        total = None
        for piece in halves(acc_buf[p]):
            part = lax.dot_general(
                ones, piece, (((1,), (1,)), ((), ())), preferred_element_type=f32
            )
            total = part if total is None else total + part
        speed_send[p] = total

    def send_speed(off, _):
        dest = lax.rem(me + off, OWNERS)
        pltpu.make_async_remote_copy(
            src_ref=speed_send.at[lax.div(dest, 8), pl.ds(0, 1)],
            dst_ref=speed_recv.at[me, pl.ds(0, 1)],
            send_sem=all_send.at[2],
            recv_sem=all_recv.at[2],
            device_id={"coef": dest},
            device_id_type=MESH,
        ).start()
        return 0

    lax.fori_loop(1, OWNERS, send_speed, 0)
    speed_recv[me, 0:1, :] = speed_send[lax.div(me, 8), 0:1, :]

    def wait_all(ref, sem):
        pltpu.make_async_copy(ref, ref, sem).wait()

    src_31 = src.at[pl.ds(0, (OWNERS - 1) * CELLS)]
    wait_all(src_31, all_recv.at[0])
    for n in (2, 3, 4, 5, 6):
        loads[n].wait()
    outer = (outer_ref[0], outer_ref[1])
    inner = (inner_ref[0], inner_ref[1])
    source = jnp.concatenate(
        [src_recv[0].reshape(256, WIDTH), src_recv[1].reshape(256, WIDTH)], axis=1
    )
    es_buf[...] = product(halves(product(outer, (source,))), inner)

    wait_all(mu_send.at[pl.ds(0, OWNERS - 1)], all_recv.at[1])
    pltpu.make_async_copy(mu_send.at[0], mu_send.at[0], local_sem.at[7]).wait()
    mu_high, mu_low = [], []
    for half in range(2):
        high_rows, low_rows = [], []
        for mode in range(NH):
            block = jnp.concatenate(
                decode(
                    mu_recv[half, mode, 0:8, :], mu_recv[half, mode, 8:9, :], weight_cube
                ),
                axis=0,
            )
            high, low = halves(block)
            high_rows.append(high)
            low_rows.append(low)
        mu_high.append(jnp.concatenate(high_rows, axis=0))
        mu_low.append(jnp.concatenate(low_rows, axis=0))
    mu_cells = (jnp.concatenate(mu_high, axis=1), jnp.concatenate(mu_low, axis=1))
    first = halves(product(outer, mu_cells))
    inner_t = (inner_t_ref[0], inner_t_ref[1])
    outer_t = (outer_t_ref[0], outer_t_ref[1])
    line, square = line_buf[...], square_buf[...]
    back = []
    for block in range(3):
        here = slice(block * 128, block * 128 + 128)
        values = product((first[0][here], first[1][here]), inner)
        u_buf[here, :] = values
        weighted = []
        for n in range(8):
            a = block * 8 + n
            u = values[n * CELLS : n * CELLS + CELLS]
            x = float(nodes[a])
            form = (square + x * (line + x * col[0])) * ratio_ref[a : a + 1, :]
            weighted.append(u + u * form)
        back.append(product(halves(jnp.concatenate(weighted, axis=0)), inner_t))
    adj = product(outer_t, halves(jnp.concatenate(back, axis=0)))
    for mode in range(NH):
        for half in range(2):
            dest = 2 * mode + half
            block = adj[mode * CELLS : mode * CELLS + CELLS, half * WIDTH : half * WIDTH + WIDTH]
            word, level = encode(block[0:8], block[8:16])
            back_send[dest, 0:8, :] = word
            back_send[dest, 8:9, :] = level

    def send_back(off, _):
        dest = lax.rem(me + off, OWNERS)
        pltpu.make_async_remote_copy(
            src_ref=back_send.at[dest],
            dst_ref=back_recv.at[me],
            send_sem=all_send.at[3],
            recv_sem=all_recv.at[3],
            device_id={"coef": dest},
            device_id_type=MESH,
        ).start()
        return 0

    lax.fori_loop(1, OWNERS, send_back, 0)
    own_back = pltpu.make_async_copy(back_send.at[me], back_recv.at[me], local_sem.at[8])
    own_back.start()

    sums = [None, None, None]
    for a in range(QP):
        here = slice(a * CELLS, a * CELLS + CELLS)
        y = u_buf[here, :] * es_buf[here, :] * ratio_ref[a : a + 1, :]
        x = float(nodes[a])
        for n, term in enumerate((y, x * y, (x * x) * y)):
            sums[n] = term if sums[n] is None else sums[n] + term
    strain_sum = None
    for n in range(3):
        part = lax.dot_general(
            moments_ref[n],
            sums[n],
            (((1,), (1,)), ((), ())),
            precision=lax.Precision.HIGHEST,
            preferred_element_type=f32,
        )
        strain_sum = part if strain_sum is None else strain_sum + part
    out_strain[...] = strain_sum[0:9, :]

    wait_all(speed_recv.at[pl.ds(0, OWNERS - 1), pl.ds(0, 1)], all_recv.at[2])
    total = speed_recv[0, 0:1, :]
    for n in range(1, OWNERS):
        total = total + speed_recv[n, 0:1, :]
    start = lax.rem(me, 8) * CELLS
    total = pltpu.roll(jnp.broadcast_to(total, (8, 128)), lax.rem(128 - start, 128), 1)
    out_courant[...] = total[0:1, 0:CELLS] * (-1.0 / math.sqrt(K))

    own_back.wait()
    wait_all(back_send.at[pl.ds(0, OWNERS - 1)], all_recv.at[3])
    for n in range(OWNERS):
        low, high = decode(back_recv[n, 0:8, :], back_recv[n, 8:9, :], 1.0)
        out_source[n * CELLS : n * CELLS + 8, :] = low
        out_source[n * CELLS + 8 : n * CELLS + 16, :] = high

    wait_all(src_31, all_send.at[0])
    wait_all(mu_send.at[pl.ds(0, OWNERS - 1)], all_send.at[1])
    wait_all(speed_recv.at[pl.ds(0, OWNERS - 1), pl.ds(0, 1)], all_send.at[2])
    wait_all(back_send.at[pl.ds(0, OWNERS - 1)], all_send.at[3])


def body(cotangent, transport_state, source_state, courant, upwind_codes, strain_rate):
    nodes, *constants = tables()
    rows = PLANES * CYZ
    anywhere = pl.BlockSpec(memory_space=pl.ANY)
    vmem = pl.BlockSpec(memory_space=pltpu.VMEM)
    adj_source, adj_strain, adj_courant = pl.pallas_call(
        functools.partial(kernel, nodes),
        out_shape=(
            jax.ShapeDtypeStruct((rows, WIDTH), f32),
            jax.ShapeDtypeStruct((9, CELLS), f32),
            jax.ShapeDtypeStruct((1, CELLS), f32),
        ),
        in_specs=[anywhere] * 3 + [vmem] * 3 + [anywhere] * 4 + [vmem] * 3,
        out_specs=(vmem, vmem, vmem),
        scratch_shapes=[
            pltpu.VMEM((3 * rows, WIDTH), f32),
            pltpu.VMEM((3 * rows, WIDTH), bf16),
            pltpu.VMEM((3, PLANES, CYZ), f32),
            pltpu.VMEM((128, 128), f32),
            pltpu.VMEM((PLANES, CYZ, WIDTH), f32),
            pltpu.VMEM((2, NH, CELLS, WIDTH), bf16),
            pltpu.VMEM((OWNERS, 9, WIDTH), jnp.int32),
            pltpu.VMEM((2, NH, 9, WIDTH), jnp.int32),
            pltpu.VMEM((OWNERS, 9, WIDTH), jnp.int32),
            pltpu.VMEM((OWNERS, 9, WIDTH), jnp.int32),
            pltpu.VMEM((PLANES, 8, WIDTH), f32),
            pltpu.VMEM((OWNERS, 8, WIDTH), f32),
            pltpu.VMEM((2, QP * CELLS, NH * CELLS), bf16),
            pltpu.VMEM((2, NH * NH, POINTS), bf16),
            pltpu.VMEM((2, POINTS, NH * NH), bf16),
            pltpu.VMEM((2, NH * CELLS, QP * CELLS), bf16),
            pltpu.VMEM((QP * CELLS, POINTS), f32),
            pltpu.VMEM((QP * CELLS, POINTS), f32),
            pltpu.VMEM((CELLS, POINTS), f32),
            pltpu.VMEM((CELLS, POINTS), f32),
            pltpu.VMEM((128, 128), f32),
            pltpu.SemaphoreType.DMA((9,)),
            pltpu.SemaphoreType.DMA((2, 3)),
            pltpu.SemaphoreType.DMA((2, 3)),
            pltpu.SemaphoreType.DMA((4,)),
            pltpu.SemaphoreType.DMA((4,)),
        ],
        compiler_params=pltpu.CompilerParams(
            collective_id=0, has_side_effects=True, vmem_limit_bytes=40 * 2**20
        ),
    )(
        cotangent,
        transport_state,
        source_state,
        courant.reshape(PLANES, CYZ),
        upwind_codes.reshape(PLANES, CYZ),
        strain_rate,
        *[jnp.asarray(table) for table in constants],
    )
    return adj_source, adj_strain, adj_courant.reshape(CELLS)


def solution(mesh):
    placed = (
        P("slab", "coef"),
        P("slab", "coef"),
        P("slab", "coef"),
        P("slab"),
        P("slab"),
        P(None, ("slab", "coef")),
    )
    return jax.shard_map(
        body,
        mesh=mesh,
        in_specs=placed,
        out_specs=(P("slab", "coef"), P(None, ("slab", "coef")), P(("slab", "coef"))),
        check_vma=False,
    )
```

```python
import functools
import math

import jax
import jax.numpy as jnp
import ml_dtypes
import numpy as np
from jax import lax
from jax.experimental import pallas as pl
from jax.experimental.pallas import tpu as pltpu
from jax.sharding import PartitionSpec as P

CYZ = 128
NH = 16
QP = 24
K = 4096
PLANES = 4
SLABS = 16
OWNERS = 32
CELLS = 16
WIDTH = 128
POINTS = QP * QP

section_weights = (0.25, 1.0 / 3.0, 0.5, 1.0)
quad_half = 4.5
fene_limit = 64.0
time_step = 0.005
weight_cube = (2.0 * quad_half / QP) ** 3
code_top = 32600.0
f32 = jnp.float32
bf16 = jnp.bfloat16
MESH = pl.DeviceIdType.MESH


def split_table(table):
    high = table.astype(np.float32).astype(ml_dtypes.bfloat16)
    low = (table - high.astype(np.float64)).astype(np.float32).astype(ml_dtypes.bfloat16)
    return np.stack([high, low])


@functools.cache
def tables():
    x = quad_half * (2.0 * np.arange(QP) + 1.0 - QP) / QP
    rows = [np.exp(-0.5 * x * x) * math.pi ** (-0.25)]
    rows.append(math.sqrt(2.0) * x * rows[0])
    for m in range(1, NH - 1):
        rows.append(
            math.sqrt(2.0 / (m + 1.0)) * x * rows[m] - math.sqrt(m / (m + 1.0)) * rows[m - 1]
        )
    h = np.stack(rows)
    inner = np.kron(h, h)
    outer = np.kron(h.T, np.eye(CELLS))
    xb = np.repeat(x, QP)
    xd = np.tile(x, QP)
    square = x[:, None] ** 2 + (xb**2 + xd**2)[None, :]
    ratio = time_step / (1.0 - square / fene_limit)
    zero = np.zeros(POINTS)
    one = np.ones(POINTS)
    moments = np.zeros((3, 16, POINTS))
    moments[0, [4, 5, 7, 8]] = [xb * xb, xb * xd, xb * xd, xd * xd]
    moments[1, [1, 2, 3, 6]] = [xb, xd, xb, xd]
    moments[2, 0] = one
    points = np.stack([xb, xd, xb * xb, xb * xd, xd * xd, zero, zero, zero])
    return (
        x,
        split_table(outer),
        split_table(inner),
        split_table(np.ascontiguousarray(inner.T)),
        split_table(np.ascontiguousarray(outer.T)),
        ratio.astype(np.float32),
        points.astype(np.float32),
        moments.astype(np.float32),
    )


def halves(value):
    high = value.astype(bf16)
    return high, (value - high.astype(f32)).astype(bf16)


def product(left, right):
    total = None
    for i, a in enumerate(left):
        for j, b in enumerate(right):
            if i + j < 2:
                part = jnp.dot(a, b, preferred_element_type=f32)
                total = part if total is None else total + part
    return total


def encode(low, high):
    top = jnp.max(jnp.maximum(jnp.abs(low), jnp.abs(high)), axis=0, keepdims=True)
    level = jnp.ceil(jnp.log2(jnp.maximum(top, 1e-30)) * 8.0)
    unit = jnp.exp2(level * -0.125) * code_top
    low_code = jnp.round(low * unit).astype(jnp.int32)
    high_code = jnp.round(high * unit).astype(jnp.int32)
    word = jnp.bitwise_or(lax.shift_left(high_code, 16), jnp.bitwise_and(low_code, 0xFFFF))
    return word, level.astype(jnp.int32)


def decode(word, level, factor):
    unit = jnp.exp2(level.astype(f32) * 0.125) * (factor / code_top)
    low = lax.shift_right_arithmetic(lax.shift_left(word, 16), 16).astype(f32) * unit
    high = lax.shift_right_arithmetic(word, 16).astype(f32) * unit
    return low, high


def sum_code(value):
    size = jnp.abs(value)
    code = jnp.round((jnp.log2(jnp.maximum(size, 1e-30)) + 100.0) * 2.0**20).astype(jnp.int32)
    code = jnp.where(size < 1e-30, 0, code)
    return jnp.where(value < 0.0, -code, code)


def sum_value(code):
    size = jnp.exp2(jnp.abs(code).astype(f32) * 2.0**-20 - 100.0)
    size = jnp.where(code == 0, 0.0, size)
    return jnp.where(code < 0, -size, size)


def kernel(
    nodes,
    cot, tst, src, cou_hbm, cod_hbm, strain_hbm,
    outer_hbm, inner_hbm, inner_t_hbm, outer_t_hbm, ratio_hbm, points_hbm, moments_hbm,
    back_recv, out_strain, out_courant,
    gbuf, tbuf, scbuf, sct_buf,
    src_recv, mu_send, mu_recv, back_send,
    cou, cod, strain,
    outer_ref, inner_ref, inner_t_ref, outer_t_ref, ratio_ref, points_ref, moments_ref,
    u_buf, es_buf, square_buf, line_buf, column_buf, strain_buf, courant_buf, courant_out,
    local_sem, halo_send, halo_recv, all_send, all_recv,
):
    me = lax.axis_index("coef")
    slab = lax.axis_index("slab")
    above = lax.rem(slab + 1, SLABS)
    below = lax.rem(slab + SLABS - 1, SLABS)
    my_x, my_z = lax.div(me, 16), lax.rem(me, 16)
    my_half, my_mode = lax.rem(me, 2), lax.div(me, 2)
    own = pl.ds(PLANES, PLANES)

    loads = [
        pltpu.make_async_copy(cot, gbuf.at[own], local_sem.at[0]),
        pltpu.make_async_copy(tst, tbuf.at[own], local_sem.at[1]),
        pltpu.make_async_copy(outer_hbm, outer_ref, local_sem.at[2]),
        pltpu.make_async_copy(inner_hbm, inner_ref, local_sem.at[3]),
        pltpu.make_async_copy(inner_t_hbm, inner_t_ref, local_sem.at[4]),
        pltpu.make_async_copy(outer_t_hbm, outer_t_ref, local_sem.at[5]),
        pltpu.make_async_copy(
            src.at[pl.ds(pl.multiple_of(me * CELLS, CELLS), CELLS)],
            src_recv.at[my_half, my_mode],
            local_sem.at[6],
        ),
        pltpu.make_async_copy(cou_hbm, cou, local_sem.at[9]),
        pltpu.make_async_copy(cod_hbm, cod, local_sem.at[10]),
        pltpu.make_async_copy(strain_hbm, strain, local_sem.at[11]),
        pltpu.make_async_copy(ratio_hbm, ratio_ref, local_sem.at[12]),
        pltpu.make_async_copy(points_hbm, points_ref, local_sem.at[13]),
        pltpu.make_async_copy(moments_hbm, moments_ref, local_sem.at[14]),
    ]
    barrier = pltpu.get_barrier_semaphore()

    def greet(off, _):
        pl.semaphore_signal(
            barrier, inc=1, device_id={"coef": lax.rem(me + off, OWNERS)}, device_id_type=MESH
        )
        return 0

    pl.semaphore_signal(barrier, inc=1, device_id={"slab": above}, device_id_type=MESH)
    pl.semaphore_signal(barrier, inc=1, device_id={"slab": below}, device_id_type=MESH)
    lax.fori_loop(1, OWNERS, greet, 0)
    for n in (7, 8, 9, 0, 1, 6, 11, 2, 3, 4, 5, 10, 12):
        loads[n].start()
    loads[7].wait()
    loads[8].wait()
    scbuf[1] = jnp.where(cod[...] == 1, -cou[...], cou[...])
    pl.semaphore_wait(barrier, OWNERS + 1)

    def halo_copy(way, kind, part):
        target, place = ((above, 0), (below, 2))[way]
        if kind == 0:
            source, dest, sem = scbuf.at[1], scbuf.at[place], 0
        else:
            rows = pl.ds(pl.multiple_of(part * 32, 32), 32)
            planes = pl.ds(place * PLANES, PLANES)
            held, buf = ((tst, tbuf), (cot, gbuf))[kind - 1]
            source, dest, sem = held.at[:, rows], buf.at[planes, rows], 4 * kind - 3 + part
        return pltpu.make_async_remote_copy(
            src_ref=source,
            dst_ref=dest,
            send_sem=halo_send.at[way, sem],
            recv_sem=halo_recv.at[way, sem],
            device_id={"slab": target},
            device_id_type=MESH,
        )

    first_part = lax.div(lax.rem(me, 8), 2)
    order = [lax.rem(first_part + n, 4) for n in (0, 1, 3, 2)]
    for way in range(2):
        halo_copy(way, 0, 0).start()
    for part in order:
        for kind in (1, 2):
            for way in range(2):
                halo_copy(way, kind, part).start()

    loads[9].wait()
    loads[11].wait()
    column_buf[...] = jnp.zeros((128, 128), f32)
    column_buf[0:9, 0:16] = strain[...]
    strain_turned = jnp.transpose(column_buf[...])[0:16]
    col = [strain_turned[:, p : p + 1] for p in range(9)]
    pts = [points_ref[n : n + 1] for n in range(5)]
    line_buf[...] = (col[1] + col[3]) * pts[0] + (col[2] + col[6]) * pts[1]
    square_buf[...] = col[4] * pts[2] + (col[5] + col[7]) * pts[3] + col[8] * pts[4]

    loads[0].wait()
    loads[1].wait()
    for way in range(2):
        halo_copy(way, 0, 0).wait()
    signed = jnp.concatenate([scbuf[0], scbuf[1], scbuf[2], jnp.zeros((116, 128), f32)], axis=0)
    sct_buf[...] = jnp.transpose(signed)
    ones = jnp.ones((8, WIDTH), bf16)

    def chunk(part):
        mu_parts, acc_parts = [], []
        for h in range(2):
            y = pl.multiple_of(part * 16 + h * 8, 8)
            sct = sct_buf[pl.ds(y, 8), :]
            wide = [jnp.broadcast_to(sct[:, p : p + 1], (8, WIDTH)) for p in range(12)]
            upper = [c < 0.0 for c in wide]
            c0 = [jnp.maximum(c, 0.0) for c in wide]
            c1 = [jnp.maximum(-c, 0.0) for c in wide]
            speed = [jnp.abs(c) for c in wide]
            s0 = [
                tbuf[p, pl.ds(pl.multiple_of(part * 16, 16), 16), :].astype(f32)[h * 8 : h * 8 + 8]
                for p in range(12)
            ]
            s = dict(enumerate(s0))
            own_change = []
            for n in range(4):
                edge = {p: s[p + 1] - s[p] for p in range(n, 11 - n)}
                change = {p: jnp.where(upper[p], edge[p], edge[p - 1]) for p in range(n + 1, 11 - n)}
                own_change.append([change[p] for p in range(4, 8)])
                if n < 3:
                    s = {p: s0[p] - section_weights[n] * speed[p] * change[p] for p in change}
            g = {p: gbuf[p, pl.ds(y, 8), :] for p in range(12)}
            mu = [g[p] for p in range(4, 8)]
            acc = [None] * 4
            for k, n in enumerate((3, 2, 1, 0)):
                for p in range(4):
                    term = section_weights[n] * (g[p + 4] * own_change[n][p])
                    acc[p] = term if acc[p] is None else acc[p] + term
                flow = {p: c1[p] * g[p] + c0[p + 1] * g[p + 1] for p in range(k, 11 - k)}
                g = {p: section_weights[n] * (flow[p] - flow[p - 1]) for p in range(k + 1, 11 - k)}
                mu = [mu[p] + g[p + 4] for p in range(4)]
            mu_parts.append(mu)
            acc_parts.append(acc)
        stack = jnp.concatenate([acc_parts[h][p] for p in range(4) for h in range(2)], axis=0)
        total = None
        for piece in halves(stack):
            term = lax.dot_general(
                ones, piece, (((1,), (1,)), ((), ())), preferred_element_type=f32
            )
            total = term if total is None else total + term
        codes = sum_code(total[0:1, :])
        for p in range(4):
            dest = p * 8 + part
            word, level = encode(mu_parts[0][p], mu_parts[1][p])
            mu_send[dest, 0:8, :] = word
            mu_send[dest, 8:9, :] = level
            mu_send[dest, 9:10, 0 : 4 * CELLS] = codes
            where_to = mu_recv.at[my_half, my_mode]

            @pl.when(dest != me)
            def _():
                pltpu.make_async_remote_copy(
                    src_ref=mu_send.at[dest],
                    dst_ref=where_to,
                    send_sem=all_send.at[1],
                    recv_sem=all_recv.at[1],
                    device_id={"coef": dest},
                    device_id_type=MESH,
                ).start()

            @pl.when(dest == me)
            def _():
                pltpu.make_async_copy(mu_send.at[dest], where_to, local_sem.at[7]).start()

    def chunks(step, _):
        part = lax.rem(first_part + step + lax.div(step, 2) * (5 - 2 * step), 4)
        for kind in (1, 2):
            for way in range(2):
                halo_copy(way, kind, part).wait()

        def half(n, _):
            chunk(part * 2 + n)
            return 0

        lax.fori_loop(0, 2, half, 0)
        return 0

    lax.fori_loop(0, 4, chunks, 0)

    def send_source(off, _):
        dest = lax.rem(me + off, OWNERS)
        pltpu.make_async_remote_copy(
            src_ref=src.at[pl.ds(pl.multiple_of(dest * CELLS, CELLS), CELLS)],
            dst_ref=src_recv.at[my_half, my_mode],
            send_sem=all_send.at[0],
            recv_sem=all_recv.at[0],
            device_id={"coef": dest},
            device_id_type=MESH,
        ).start()
        return 0

    lax.fori_loop(1, OWNERS, send_source, 0)

    def wait_all(ref, sem):
        pltpu.make_async_copy(ref, ref, sem).wait()

    src_31 = src.at[pl.ds(0, (OWNERS - 1) * CELLS)]
    for n in (2, 3, 4, 5, 6, 10, 12):
        loads[n].wait()
    outer = (outer_ref[0], outer_ref[1])
    inner = (inner_ref[0], inner_ref[1])

    wait_all(mu_send.at[pl.ds(0, OWNERS - 1)], all_recv.at[1])
    pltpu.make_async_copy(mu_send.at[0], mu_send.at[0], local_sem.at[7]).wait()
    mu_high, mu_low = [], []
    for half in range(2):
        high_rows, low_rows = [], []
        for mode in range(NH):
            block = jnp.concatenate(
                decode(
                    mu_recv[half, mode, 0:8, :], mu_recv[half, mode, 8:9, :], weight_cube
                ),
                axis=0,
            )
            high, low = halves(block)
            high_rows.append(high)
            low_rows.append(low)
        mu_high.append(jnp.concatenate(high_rows, axis=0))
        mu_low.append(jnp.concatenate(low_rows, axis=0))
    mu_cells = (jnp.concatenate(mu_high, axis=1), jnp.concatenate(mu_low, axis=1))
    first = halves(product(outer, mu_cells))
    inner_t = (inner_t_ref[0], inner_t_ref[1])
    outer_t = (outer_t_ref[0], outer_t_ref[1])
    line, square = line_buf[...], square_buf[...]
    back = []
    for block in range(3):
        here = slice(block * 128, block * 128 + 128)
        values = product((first[0][here], first[1][here]), inner)
        u_buf[here, :] = values
        weighted = []
        for n in range(8):
            a = block * 8 + n
            u = values[n * CELLS : n * CELLS + CELLS]
            x = float(nodes[a])
            form = (square + x * (line + x * col[0])) * ratio_ref[a : a + 1, :]
            weighted.append(u + u * form)
        back.append(product(halves(jnp.concatenate(weighted, axis=0)), inner_t))
    adj = product(outer_t, halves(jnp.concatenate(back, axis=0)))
    for mode in range(NH):
        for half in range(2):
            dest = 2 * mode + half
            block = adj[mode * CELLS : mode * CELLS + CELLS, half * WIDTH : half * WIDTH + WIDTH]
            word, level = encode(block[0:8], block[8:16])
            back_send[dest, 0:8, :] = word
            back_send[dest, 8:9, :] = level

    def send_back(step, _):
        z = lax.div(step, 2)
        late = z - 8
        z = jnp.where(z < 8, z, jnp.where(z < 12, 15 - late, late + 4))
        dest = lax.rem(step, 2) * 16 + z

        @pl.when(dest != me)
        def _():
            pltpu.make_async_remote_copy(
                src_ref=back_send.at[dest],
                dst_ref=back_recv.at[me],
                send_sem=all_send.at[3],
                recv_sem=all_recv.at[3],
                device_id={"coef": dest},
                device_id_type=MESH,
            ).start()

        return 0

    lax.fori_loop(0, OWNERS, send_back, 0)
    own_back = pltpu.make_async_copy(back_send.at[me], back_recv.at[me], local_sem.at[8])
    own_back.start()

    total = None
    for half in range(2):
        for mode in range(NH):
            row = sum_value(mu_recv[half, mode, 9:10, 0 : 4 * CELLS])
            total = row if total is None else total + row
    courant_buf[...] = jnp.zeros((8, 128), f32)
    courant_buf[0:1, 0 : 4 * CELLS] = total
    turn = lax.rem(128 - lax.div(me, 8) * CELLS, 128)
    turned = pltpu.roll(courant_buf[...], turn, 1) * (-1.0 / math.sqrt(K))
    courant_out[...] = turned[0:1, 0:CELLS]
    outs = [pltpu.make_async_copy(courant_out, out_courant, local_sem.at[15])]
    outs[0].start()

    wait_all(src_31, all_recv.at[0])
    source = jnp.concatenate(
        [src_recv[0].reshape(256, WIDTH), src_recv[1].reshape(256, WIDTH)], axis=1
    )
    es_buf[...] = product(halves(product(outer, (source,))), inner)
    sums = [None, None, None]
    for a in range(QP):
        here = slice(a * CELLS, a * CELLS + CELLS)
        y = u_buf[here, :] * es_buf[here, :] * ratio_ref[a : a + 1, :]
        x = float(nodes[a])
        for n, term in enumerate((y, x * y, (x * x) * y)):
            sums[n] = term if sums[n] is None else sums[n] + term
    strain_sum = None
    for n in range(3):
        part = lax.dot_general(
            moments_ref[n],
            sums[n],
            (((1,), (1,)), ((), ())),
            precision=lax.Precision.HIGHEST,
            preferred_element_type=f32,
        )
        strain_sum = part if strain_sum is None else strain_sum + part
    strain_buf[...] = strain_sum[0:9, :]
    outs.append(pltpu.make_async_copy(strain_buf, out_strain, local_sem.at[16]))
    outs[1].start()

    own_back.wait()
    for copy in outs:
        copy.wait()
    wait_all(src_31, all_send.at[0])
    wait_all(mu_send.at[pl.ds(0, OWNERS - 1)], all_send.at[1])
    wait_all(back_send.at[pl.ds(0, OWNERS - 1)], all_send.at[3])
    wait_all(back_send.at[pl.ds(0, OWNERS - 1)], all_recv.at[3])


def finish(
    back_hbm, strain_hbm, courant_hbm, out_source, out_strain, out_courant, back, source, sem
):
    small = [
        pltpu.make_async_copy(strain_hbm, out_strain, sem.at[0]),
        pltpu.make_async_copy(courant_hbm, out_courant, sem.at[1]),
    ]
    load = pltpu.make_async_copy(back_hbm, back, sem.at[2])
    load.start()
    for copy in small:
        copy.start()
    load.wait()
    stores = []
    for part in range(2):
        for n in range(part * 16, part * 16 + 16):
            low, high = decode(back[n, 0:8, :], back[n, 8:9, :], 1.0)
            source[n * CELLS : n * CELLS + 8, :] = low
            source[n * CELLS + 8 : n * CELLS + 16, :] = high
        here = pl.ds(part * 256, 256)
        stores.append(pltpu.make_async_copy(source.at[here], out_source.at[here], sem.at[3 + part]))
        stores[-1].start()
    for copy in small + stores:
        copy.wait()


def body(cotangent, transport_state, source_state, courant, upwind_codes, strain_rate):
    nodes, *constants = tables()
    rows = PLANES * CYZ
    hbm = pl.BlockSpec(memory_space=pltpu.HBM)
    results = pl.pallas_call(
        functools.partial(kernel, nodes),
        out_shape=(
            jax.ShapeDtypeStruct((OWNERS, 9, WIDTH), jnp.int32),
            jax.ShapeDtypeStruct((9, CELLS), f32),
            jax.ShapeDtypeStruct((1, CELLS), f32),
        ),
        in_specs=[hbm] * 13,
        out_specs=[hbm] * 3,
        scratch_shapes=[
            pltpu.VMEM((3 * PLANES, CYZ, WIDTH), f32),
            pltpu.VMEM((3 * PLANES, CYZ, WIDTH), bf16),
            pltpu.VMEM((3, PLANES, CYZ), f32),
            pltpu.VMEM((128, 128), f32),
            pltpu.VMEM((2, NH, CELLS, WIDTH), bf16),
            pltpu.VMEM((OWNERS, 10, WIDTH), jnp.int32),
            pltpu.VMEM((2, NH, 10, WIDTH), jnp.int32),
            pltpu.VMEM((OWNERS, 9, WIDTH), jnp.int32),
            pltpu.VMEM((PLANES, CYZ), f32),
            pltpu.VMEM((PLANES, CYZ), jnp.int32),
            pltpu.VMEM((9, CELLS), f32),
            pltpu.VMEM((2, QP * CELLS, NH * CELLS), bf16),
            pltpu.VMEM((2, NH * NH, POINTS), bf16),
            pltpu.VMEM((2, POINTS, NH * NH), bf16),
            pltpu.VMEM((2, NH * CELLS, QP * CELLS), bf16),
            pltpu.VMEM((QP, POINTS), f32),
            pltpu.VMEM((8, POINTS), f32),
            pltpu.VMEM((3, 16, POINTS), f32),
            pltpu.VMEM((QP * CELLS, POINTS), f32),
            pltpu.VMEM((QP * CELLS, POINTS), f32),
            pltpu.VMEM((CELLS, POINTS), f32),
            pltpu.VMEM((CELLS, POINTS), f32),
            pltpu.VMEM((128, 128), f32),
            pltpu.VMEM((9, CELLS), f32),
            pltpu.VMEM((8, WIDTH), f32),
            pltpu.VMEM((1, CELLS), f32),
            pltpu.SemaphoreType.DMA((17,)),
            pltpu.SemaphoreType.DMA((2, 9)),
            pltpu.SemaphoreType.DMA((2, 9)),
            pltpu.SemaphoreType.DMA((4,)),
            pltpu.SemaphoreType.DMA((4,)),
        ],
        compiler_params=pltpu.CompilerParams(
            collective_id=0, has_side_effects=True, vmem_limit_bytes=60 * 2**20
        ),
    )(
        cotangent.reshape(PLANES, CYZ, WIDTH),
        transport_state.reshape(PLANES, CYZ, WIDTH),
        source_state,
        courant.reshape(PLANES, CYZ),
        upwind_codes.reshape(PLANES, CYZ),
        strain_rate,
        *[jnp.asarray(table) for table in constants],
    )
    adj_source, adj_strain, adj_courant = pl.pallas_call(
        finish,
        out_shape=(
            jax.ShapeDtypeStruct((rows, WIDTH), f32),
            jax.ShapeDtypeStruct((9, CELLS), f32),
            jax.ShapeDtypeStruct((1, CELLS), f32),
        ),
        in_specs=[hbm] * 3,
        out_specs=[hbm] * 3,
        scratch_shapes=[
            pltpu.VMEM((OWNERS, 9, WIDTH), jnp.int32),
            pltpu.VMEM((rows, WIDTH), f32),
            pltpu.SemaphoreType.DMA((5,)),
        ],
        compiler_params=pltpu.CompilerParams(vmem_limit_bytes=60 * 2**20),
    )(*results)
    return adj_source, adj_strain, adj_courant.reshape(CELLS)


def solution(mesh):
    placed = (
        P("slab", "coef"),
        P("slab", "coef"),
        P("slab", "coef"),
        P("slab"),
        P("slab"),
        P(None, ("slab", "coef")),
    )
    return jax.shard_map(
        body,
        mesh=mesh,
        in_specs=placed,
        out_specs=(P("slab", "coef"), P(None, ("slab", "coef")), P(("slab", "coef"))),
        check_vma=False,
    )
```

```python
import functools
import math

import jax
import jax.numpy as jnp
import ml_dtypes
import numpy as np
from jax import lax
from jax.experimental import pallas as pl
from jax.experimental.pallas import tpu as pltpu
from jax.sharding import PartitionSpec as P

CYZ = 128
NH = 16
QP = 24
K = 4096
PLANES = 4
SLABS = 16
OWNERS = 32
CELLS = 16
WIDTH = 128
POINTS = QP * QP

section_weights = (0.25, 1.0 / 3.0, 0.5, 1.0)
quad_half = 4.5
fene_limit = 64.0
time_step = 0.005
weight_cube = (2.0 * quad_half / QP) ** 3
code_top = 32600.0
f32 = jnp.float32
bf16 = jnp.bfloat16
MESH = pl.DeviceIdType.MESH

away_order = (8, 7, -7, 6, -6, 5, -5, 4, -4, 3, -3, 2, -2, 1, -1, 0)
far = [(away, other) for away in away_order[:7] for other in (1, 0)]
near = [(away, other) for away in away_order[7:] for other in (1, 0) if (away, other) != (0, 0)]


def split_table(table):
    high = table.astype(np.float32).astype(ml_dtypes.bfloat16)
    low = (table - high.astype(np.float64)).astype(np.float32).astype(ml_dtypes.bfloat16)
    return np.stack([high, low])


@functools.cache
def tables():
    x = quad_half * (2.0 * np.arange(QP) + 1.0 - QP) / QP
    rows = [np.exp(-0.5 * x * x) * math.pi ** (-0.25)]
    rows.append(math.sqrt(2.0) * x * rows[0])
    for m in range(1, NH - 1):
        rows.append(
            math.sqrt(2.0 / (m + 1.0)) * x * rows[m] - math.sqrt(m / (m + 1.0)) * rows[m - 1]
        )
    h = np.stack(rows)
    inner = np.kron(h, h)
    outer = np.kron(h.T, np.eye(CELLS))
    xb = np.repeat(x, QP)
    xd = np.tile(x, QP)
    square = x[:, None] ** 2 + (xb**2 + xd**2)[None, :]
    ratio = time_step / (1.0 - square / fene_limit)
    zero = np.zeros(POINTS)
    one = np.ones(POINTS)
    moments = np.zeros((3, 16, POINTS))
    moments[0, [4, 5, 7, 8]] = [xb * xb, xb * xd, xb * xd, xd * xd]
    moments[1, [1, 2, 3, 6]] = [xb, xd, xb, xd]
    moments[2, 0] = one
    points = np.stack([xb, xd, xb * xb, xb * xd, xd * xd, zero, zero, zero])
    return (
        x,
        split_table(outer),
        split_table(inner),
        split_table(np.ascontiguousarray(inner.T)),
        split_table(np.ascontiguousarray(outer.T)),
        ratio.astype(np.float32),
        points.astype(np.float32),
        moments.astype(np.float32),
    )


def halves(value):
    high = value.astype(bf16)
    return high, (value - high.astype(f32)).astype(bf16)


def product(left, right):
    total = None
    for i, a in enumerate(left):
        for j, b in enumerate(right):
            if i + j < 2:
                part = jnp.dot(a, b, preferred_element_type=f32)
                total = part if total is None else total + part
    return total


def encode(low, high):
    top = jnp.max(jnp.maximum(jnp.abs(low), jnp.abs(high)), axis=0, keepdims=True)
    level = jnp.ceil(jnp.log2(jnp.maximum(top, 1e-30)) * 8.0)
    unit = jnp.exp2(level * -0.125) * code_top
    low_code = jnp.round(low * unit).astype(jnp.int32)
    high_code = jnp.round(high * unit).astype(jnp.int32)
    word = jnp.bitwise_or(lax.shift_left(high_code, 16), jnp.bitwise_and(low_code, 0xFFFF))
    return word, level.astype(jnp.int32)


def decode(word, level, factor):
    unit = jnp.exp2(level.astype(f32) * 0.125) * (factor / code_top)
    low = lax.shift_right_arithmetic(lax.shift_left(word, 16), 16).astype(f32) * unit
    high = lax.shift_right_arithmetic(word, 16).astype(f32) * unit
    return low, high


def sum_code(value):
    size = jnp.abs(value)
    code = jnp.round((jnp.log2(jnp.maximum(size, 1e-30)) + 100.0) * 2.0**20).astype(jnp.int32)
    code = jnp.where(size < 1e-30, 0, code)
    return jnp.where(value < 0.0, -code, code)


def sum_value(code):
    size = jnp.exp2(jnp.abs(code).astype(f32) * 2.0**-20 - 100.0)
    size = jnp.where(code == 0, 0.0, size)
    return jnp.where(code < 0, -size, size)


def kernel(
    nodes,
    cot, tst, src, cou_hbm, cod_hbm, strain_hbm,
    outer_hbm, inner_hbm, inner_t_hbm, outer_t_hbm, ratio_hbm, points_hbm, moments_hbm,
    back_recv, out_strain, out_courant,
    gbuf, tbuf, scbuf, sct_buf, code_send, code_recv,
    src_recv, mu_send, mu_recv, back_send,
    cou, cod, strain,
    outer_ref, inner_ref, inner_t_ref, outer_t_ref, ratio_ref, points_ref, moments_ref,
    u_buf, es_buf, square_buf, line_buf, column_buf, strain_buf, courant_buf, courant_out,
    local_sem, halo_send, halo_recv, all_send, all_recv, near_sem,
):
    me = lax.axis_index("coef")
    slab = lax.axis_index("slab")
    above = lax.rem(slab + 1, SLABS)
    below = lax.rem(slab + SLABS - 1, SLABS)
    my_x, my_z = lax.div(me, 16), lax.rem(me, 16)
    my_half, my_mode = lax.rem(me, 2), lax.div(me, 2)
    own = pl.ds(PLANES, PLANES)

    loads = [
        pltpu.make_async_copy(cot, gbuf, local_sem.at[0]),
        pltpu.make_async_copy(tst, tbuf.at[own], local_sem.at[1]),
        pltpu.make_async_copy(outer_hbm, outer_ref, local_sem.at[2]),
        pltpu.make_async_copy(inner_hbm, inner_ref, local_sem.at[3]),
        pltpu.make_async_copy(inner_t_hbm, inner_t_ref, local_sem.at[4]),
        pltpu.make_async_copy(outer_t_hbm, outer_t_ref, local_sem.at[5]),
        pltpu.make_async_copy(
            src.at[pl.ds(pl.multiple_of(me * CELLS, CELLS), CELLS)],
            src_recv.at[my_half, my_mode],
            local_sem.at[6],
        ),
        pltpu.make_async_copy(cou_hbm, cou, local_sem.at[9]),
        pltpu.make_async_copy(cod_hbm, cod, local_sem.at[10]),
        pltpu.make_async_copy(strain_hbm, strain, local_sem.at[11]),
        pltpu.make_async_copy(ratio_hbm, ratio_ref, local_sem.at[12]),
        pltpu.make_async_copy(points_hbm, points_ref, local_sem.at[13]),
        pltpu.make_async_copy(moments_hbm, moments_ref, local_sem.at[14]),
    ]
    barrier = pltpu.get_barrier_semaphore()

    def owner(away, other):
        return lax.rem(my_x + other, 2) * 16 + lax.rem(my_z + away + 16, 16)

    def signal_near(sem):
        for away, other in near:
            pl.semaphore_signal(
                sem, inc=1, device_id={"coef": owner(away, other)}, device_id_type=MESH
            )

    pl.semaphore_signal(barrier, inc=1, device_id={"slab": above}, device_id_type=MESH)
    pl.semaphore_signal(barrier, inc=1, device_id={"slab": below}, device_id_type=MESH)
    signal_near(barrier)
    for n in (0, 7, 8, 9, 1, 6, 11, 2, 3, 4, 5, 10, 12):
        loads[n].start()
    loads[7].wait()
    loads[8].wait()
    scbuf[1] = jnp.where(cod[...] == 1, -cou[...], cou[...])
    loads[0].wait()
    for part in range(4):
        for p in range(PLANES):
            for n in range(2):
                y = part * 32 + n * 16
                word, level = encode(gbuf[p, y : y + 8, :], gbuf[p, y + 8 : y + 16, :])
                code_send[part, p * 2 + n, 0:8, :] = word
                code_send[part, p * 2 + n, 8:9, :] = level
    pl.semaphore_wait(barrier, len(near) + 2)
    signal_near(near_sem)

    def halo_copy(way, kind, part):
        target, place = ((above, 0), (below, 2))[way]
        if kind == 0:
            source, dest, sem = scbuf.at[1], scbuf.at[place], 0
        elif kind == 1:
            rows = pl.ds(pl.multiple_of(part * 32, 32), 32)
            planes = pl.ds(place * PLANES, PLANES)
            source, dest, sem = tst.at[:, rows], tbuf.at[planes, rows], 1 + part
        else:
            source, dest, sem = code_send.at[part], code_recv.at[way, part], 5 + part
        return pltpu.make_async_remote_copy(
            src_ref=source,
            dst_ref=dest,
            send_sem=halo_send.at[way, sem],
            recv_sem=halo_recv.at[way, sem],
            device_id={"slab": target},
            device_id_type=MESH,
        )

    first_part = lax.div(lax.rem(me, 8), 2)
    order = [lax.rem(first_part + n, 4) for n in (0, 1, 3, 2)]
    for way in range(2):
        halo_copy(way, 0, 0).start()
    for part in order:
        for kind in (1, 2):
            for way in range(2):
                halo_copy(way, kind, part).start()

    def send_source(away, other):
        dest = owner(away, other)
        pltpu.make_async_remote_copy(
            src_ref=src.at[pl.ds(pl.multiple_of(dest * CELLS, CELLS), CELLS)],
            dst_ref=src_recv.at[my_half, my_mode],
            send_sem=all_send.at[0],
            recv_sem=all_recv.at[0],
            device_id={"coef": dest},
            device_id_type=MESH,
        ).start()

    for away, other in near:
        send_source(away, other)

    loads[9].wait()
    loads[11].wait()
    column_buf[...] = jnp.zeros((128, 128), f32)
    column_buf[0:9, 0:16] = strain[...]
    strain_turned = jnp.transpose(column_buf[...])[0:16]
    col = [strain_turned[:, p : p + 1] for p in range(9)]
    pts = [points_ref[n : n + 1] for n in range(5)]
    line_buf[...] = (col[1] + col[3]) * pts[0] + (col[2] + col[6]) * pts[1]
    square_buf[...] = col[4] * pts[2] + (col[5] + col[7]) * pts[3] + col[8] * pts[4]

    loads[1].wait()
    for way in range(2):
        halo_copy(way, 0, 0).wait()
    signed = jnp.concatenate([scbuf[0], scbuf[1], scbuf[2], jnp.zeros((116, 128), f32)], axis=0)
    sct_buf[...] = jnp.transpose(signed)
    ones = jnp.ones((8, WIDTH), bf16)

    def chunk(quarter, n):
        part = quarter * 2 + n
        mu_parts, acc_parts = [], []
        coded = [
            (code_recv.at[way, quarter, p * 2 + n], way * 8 + p)
            for way in range(2)
            for p in range(PLANES)
        ]
        unit = {p: jnp.exp2(ref[8:9, :].astype(f32) * 0.125) * (1.0 / code_top) for ref, p in coded}
        for h in range(2):
            y = pl.multiple_of(part * 16 + h * 8, 8)
            sct = sct_buf[pl.ds(y, 8), :]
            wide = [jnp.broadcast_to(sct[:, p : p + 1], (8, WIDTH)) for p in range(12)]
            upper = [c < 0.0 for c in wide]
            c0 = [jnp.maximum(c, 0.0) for c in wide]
            c1 = [jnp.maximum(-c, 0.0) for c in wide]
            speed = [jnp.abs(c) for c in wide]
            s0 = [
                tbuf[p, pl.ds(pl.multiple_of(part * 16, 16), 16), :].astype(f32)[h * 8 : h * 8 + 8]
                for p in range(12)
            ]
            s = dict(enumerate(s0))
            own_change = []
            for n in range(4):
                edge = {p: s[p + 1] - s[p] for p in range(n, 11 - n)}
                change = {p: jnp.where(upper[p], edge[p], edge[p - 1]) for p in range(n + 1, 11 - n)}
                own_change.append([change[p] for p in range(4, 8)])
                if n < 3:
                    s = {p: s0[p] - section_weights[n] * speed[p] * change[p] for p in change}
            g = {p + 4: gbuf[p, pl.ds(y, 8), :] for p in range(PLANES)}
            for ref, p in coded:
                word = ref[0:8, :]
                if h == 0:
                    word = lax.shift_left(word, 16)
                g[p] = lax.shift_right_arithmetic(word, 16).astype(f32) * unit[p]
            mu = [g[p] for p in range(4, 8)]
            acc = [None] * 4
            for k, n in enumerate((3, 2, 1, 0)):
                for p in range(4):
                    term = section_weights[n] * (g[p + 4] * own_change[n][p])
                    acc[p] = term if acc[p] is None else acc[p] + term
                flow = {p: c1[p] * g[p] + c0[p + 1] * g[p + 1] for p in range(k, 11 - k)}
                g = {p: section_weights[n] * (flow[p] - flow[p - 1]) for p in range(k + 1, 11 - k)}
                mu = [mu[p] + g[p + 4] for p in range(4)]
            mu_parts.append(mu)
            acc_parts.append(acc)
        stack = jnp.concatenate([acc_parts[h][p] for p in range(4) for h in range(2)], axis=0)
        total = None
        for piece in halves(stack):
            term = lax.dot_general(
                ones, piece, (((1,), (1,)), ((), ())), preferred_element_type=f32
            )
            total = term if total is None else total + term
        codes = sum_code(total[0:1, :])
        for p in range(4):
            dest = p * 8 + part
            word, level = encode(mu_parts[0][p], mu_parts[1][p])
            mu_send[dest, 0:8, :] = word
            mu_send[dest, 8:9, :] = level
            mu_send[dest, 9:10, 0 : 4 * CELLS] = codes
            where_to = mu_recv.at[my_half, my_mode]

            @pl.when(dest != me)
            def _():
                pltpu.make_async_remote_copy(
                    src_ref=mu_send.at[dest],
                    dst_ref=where_to,
                    send_sem=all_send.at[1],
                    recv_sem=all_recv.at[1],
                    device_id={"coef": dest},
                    device_id_type=MESH,
                ).start()

            @pl.when(dest == me)
            def _():
                pltpu.make_async_copy(mu_send.at[dest], where_to, local_sem.at[7]).start()

    def chunks(step, _):
        part = lax.rem(first_part + step + lax.div(step, 2) * (5 - 2 * step), 4)
        for kind in (1, 2):
            for way in range(2):
                halo_copy(way, kind, part).wait()

        def half(n, _):
            chunk(part, n)
            return 0

        @pl.when(step == 0)
        def _():
            pl.semaphore_wait(near_sem, len(near))

        lax.fori_loop(0, 2, half, 0)
        return 0

    lax.fori_loop(0, 4, chunks, 0)

    for away, other in far:
        send_source(away, other)

    def wait_all(ref, sem):
        pltpu.make_async_copy(ref, ref, sem).wait()

    src_31 = src.at[pl.ds(0, (OWNERS - 1) * CELLS)]
    for n in (2, 3, 4, 5, 6, 10, 12):
        loads[n].wait()
    outer = (outer_ref[0], outer_ref[1])
    inner = (inner_ref[0], inner_ref[1])

    wait_all(mu_send.at[pl.ds(0, OWNERS - 1)], all_recv.at[1])
    pltpu.make_async_copy(mu_send.at[0], mu_send.at[0], local_sem.at[7]).wait()
    mu_high, mu_low = [], []
    for half in range(2):
        high_rows, low_rows = [], []
        for mode in range(NH):
            block = jnp.concatenate(
                decode(
                    mu_recv[half, mode, 0:8, :], mu_recv[half, mode, 8:9, :], weight_cube
                ),
                axis=0,
            )
            high, low = halves(block)
            high_rows.append(high)
            low_rows.append(low)
        mu_high.append(jnp.concatenate(high_rows, axis=0))
        mu_low.append(jnp.concatenate(low_rows, axis=0))
    mu_cells = (jnp.concatenate(mu_high, axis=1), jnp.concatenate(mu_low, axis=1))
    first = halves(product(outer, mu_cells))
    inner_t = (inner_t_ref[0], inner_t_ref[1])
    outer_t = (outer_t_ref[0], outer_t_ref[1])
    line, square = line_buf[...], square_buf[...]
    back = []
    for block in range(3):
        here = slice(block * 128, block * 128 + 128)
        values = product((first[0][here], first[1][here]), inner)
        u_buf[here, :] = values
        weighted = []
        for n in range(8):
            a = block * 8 + n
            u = values[n * CELLS : n * CELLS + CELLS]
            x = float(nodes[a])
            form = (square + x * (line + x * col[0])) * ratio_ref[a : a + 1, :]
            weighted.append(u + u * form)
        back.append(product(halves(jnp.concatenate(weighted, axis=0)), inner_t))
    adj = product(outer_t, halves(jnp.concatenate(back, axis=0)))
    for mode in range(NH):
        for half in range(2):
            dest = 2 * mode + half
            block = adj[mode * CELLS : mode * CELLS + CELLS, half * WIDTH : half * WIDTH + WIDTH]
            word, level = encode(block[0:8], block[8:16])
            back_send[dest, 0:8, :] = word
            back_send[dest, 8:9, :] = level

    def send_back(step, _):
        z = lax.div(step, 2)
        late = z - 8
        z = jnp.where(z < 8, z, jnp.where(z < 12, 15 - late, late + 4))
        dest = lax.rem(step, 2) * 16 + z

        @pl.when(dest != me)
        def _():
            pltpu.make_async_remote_copy(
                src_ref=back_send.at[dest],
                dst_ref=back_recv.at[me],
                send_sem=all_send.at[3],
                recv_sem=all_recv.at[3],
                device_id={"coef": dest},
                device_id_type=MESH,
            ).start()

        return 0

    lax.fori_loop(0, OWNERS, send_back, 0)
    own_back = pltpu.make_async_copy(back_send.at[me], back_recv.at[me], local_sem.at[8])
    own_back.start()

    total = None
    for half in range(2):
        for mode in range(NH):
            row = sum_value(mu_recv[half, mode, 9:10, 0 : 4 * CELLS])
            total = row if total is None else total + row
    courant_buf[...] = jnp.zeros((8, 128), f32)
    courant_buf[0:1, 0 : 4 * CELLS] = total
    turn = lax.rem(128 - lax.div(me, 8) * CELLS, 128)
    turned = pltpu.roll(courant_buf[...], turn, 1) * (-1.0 / math.sqrt(K))
    courant_out[...] = turned[0:1, 0:CELLS]
    outs = [pltpu.make_async_copy(courant_out, out_courant, local_sem.at[15])]
    outs[0].start()

    wait_all(src_31, all_recv.at[0])
    source = jnp.concatenate(
        [src_recv[0].reshape(256, WIDTH), src_recv[1].reshape(256, WIDTH)], axis=1
    )
    es_buf[...] = product(halves(product(outer, (source,))), inner)
    sums = [None, None, None]
    for a in range(QP):
        here = slice(a * CELLS, a * CELLS + CELLS)
        y = u_buf[here, :] * es_buf[here, :] * ratio_ref[a : a + 1, :]
        x = float(nodes[a])
        for n, term in enumerate((y, x * y, (x * x) * y)):
            sums[n] = term if sums[n] is None else sums[n] + term
    strain_sum = None
    for n in range(3):
        part = lax.dot_general(
            moments_ref[n],
            sums[n],
            (((1,), (1,)), ((), ())),
            precision=lax.Precision.HIGHEST,
            preferred_element_type=f32,
        )
        strain_sum = part if strain_sum is None else strain_sum + part
    strain_buf[...] = strain_sum[0:9, :]
    outs.append(pltpu.make_async_copy(strain_buf, out_strain, local_sem.at[16]))
    outs[1].start()

    own_back.wait()
    for copy in outs:
        copy.wait()
    wait_all(src_31, all_send.at[0])
    wait_all(mu_send.at[pl.ds(0, OWNERS - 1)], all_send.at[1])
    wait_all(back_send.at[pl.ds(0, OWNERS - 1)], all_send.at[3])
    wait_all(back_send.at[pl.ds(0, OWNERS - 1)], all_recv.at[3])


def finish(
    back_hbm, strain_hbm, courant_hbm, out_source, out_strain, out_courant, back, source, sem
):
    small = [
        pltpu.make_async_copy(strain_hbm, out_strain, sem.at[0]),
        pltpu.make_async_copy(courant_hbm, out_courant, sem.at[1]),
    ]
    loads = [
        pltpu.make_async_copy(back_hbm.at[here], back.at[here], sem.at[2 + part])
        for part, here in enumerate(pl.ds(n * 8, 8) for n in range(4))
    ]
    for copy in loads + small:
        copy.start()
    stores = []
    for part in range(4):
        loads[part].wait()
        for n in range(part * 8, part * 8 + 8):
            low, high = decode(back[n, 0:8, :], back[n, 8:9, :], 1.0)
            source[n * CELLS : n * CELLS + 8, :] = low
            source[n * CELLS + 8 : n * CELLS + 16, :] = high
        here = pl.ds(part * 128, 128)
        stores.append(pltpu.make_async_copy(source.at[here], out_source.at[here], sem.at[6 + part]))
        stores[-1].start()
    for copy in small + stores:
        copy.wait()


def body(cotangent, transport_state, source_state, courant, upwind_codes, strain_rate):
    nodes, *constants = tables()
    rows = PLANES * CYZ
    hbm = pl.BlockSpec(memory_space=pltpu.HBM)
    results = pl.pallas_call(
        functools.partial(kernel, nodes),
        out_shape=(
            jax.ShapeDtypeStruct((OWNERS, 9, WIDTH), jnp.int32),
            jax.ShapeDtypeStruct((9, CELLS), f32),
            jax.ShapeDtypeStruct((1, CELLS), f32),
        ),
        in_specs=[hbm] * 13,
        out_specs=[hbm] * 3,
        scratch_shapes=[
            pltpu.VMEM((PLANES, CYZ, WIDTH), f32),
            pltpu.VMEM((3 * PLANES, CYZ, WIDTH), bf16),
            pltpu.VMEM((3, PLANES, CYZ), f32),
            pltpu.VMEM((128, 128), f32),
            pltpu.VMEM((4, 2 * PLANES, 9, WIDTH), jnp.int32),
            pltpu.VMEM((2, 4, 2 * PLANES, 9, WIDTH), jnp.int32),
            pltpu.VMEM((2, NH, CELLS, WIDTH), bf16),
            pltpu.VMEM((OWNERS, 10, WIDTH), jnp.int32),
            pltpu.VMEM((2, NH, 10, WIDTH), jnp.int32),
            pltpu.VMEM((OWNERS, 9, WIDTH), jnp.int32),
            pltpu.VMEM((PLANES, CYZ), f32),
            pltpu.VMEM((PLANES, CYZ), jnp.int32),
            pltpu.VMEM((9, CELLS), f32),
            pltpu.VMEM((2, QP * CELLS, NH * CELLS), bf16),
            pltpu.VMEM((2, NH * NH, POINTS), bf16),
            pltpu.VMEM((2, POINTS, NH * NH), bf16),
            pltpu.VMEM((2, NH * CELLS, QP * CELLS), bf16),
            pltpu.VMEM((QP, POINTS), f32),
            pltpu.VMEM((8, POINTS), f32),
            pltpu.VMEM((3, 16, POINTS), f32),
            pltpu.VMEM((QP * CELLS, POINTS), f32),
            pltpu.VMEM((QP * CELLS, POINTS), f32),
            pltpu.VMEM((CELLS, POINTS), f32),
            pltpu.VMEM((CELLS, POINTS), f32),
            pltpu.VMEM((128, 128), f32),
            pltpu.VMEM((9, CELLS), f32),
            pltpu.VMEM((8, WIDTH), f32),
            pltpu.VMEM((1, CELLS), f32),
            pltpu.SemaphoreType.DMA((17,)),
            pltpu.SemaphoreType.DMA((2, 9)),
            pltpu.SemaphoreType.DMA((2, 9)),
            pltpu.SemaphoreType.DMA((4,)),
            pltpu.SemaphoreType.DMA((4,)),
            pltpu.SemaphoreType.REGULAR,
        ],
        compiler_params=pltpu.CompilerParams(
            collective_id=0, has_side_effects=True, vmem_limit_bytes=60 * 2**20
        ),
    )(
        cotangent.reshape(PLANES, CYZ, WIDTH),
        transport_state.reshape(PLANES, CYZ, WIDTH),
        source_state,
        courant.reshape(PLANES, CYZ),
        upwind_codes.reshape(PLANES, CYZ),
        strain_rate,
        *[jnp.asarray(table) for table in constants],
    )
    adj_source, adj_strain, adj_courant = pl.pallas_call(
        finish,
        out_shape=(
            jax.ShapeDtypeStruct((rows, WIDTH), f32),
            jax.ShapeDtypeStruct((9, CELLS), f32),
            jax.ShapeDtypeStruct((1, CELLS), f32),
        ),
        in_specs=[hbm] * 3,
        out_specs=[hbm] * 3,
        scratch_shapes=[
            pltpu.VMEM((OWNERS, 9, WIDTH), jnp.int32),
            pltpu.VMEM((rows, WIDTH), f32),
            pltpu.SemaphoreType.DMA((10,)),
        ],
        compiler_params=pltpu.CompilerParams(vmem_limit_bytes=60 * 2**20),
    )(*results)
    return adj_source, adj_strain, adj_courant.reshape(CELLS)


def solution(mesh):
    placed = (
        P("slab", "coef"),
        P("slab", "coef"),
        P("slab", "coef"),
        P("slab"),
        P("slab"),
        P(None, ("slab", "coef")),
    )
    return jax.shard_map(
        body,
        mesh=mesh,
        in_specs=placed,
        out_specs=(P("slab", "coef"), P(None, ("slab", "coef")), P(("slab", "coef"))),
        check_vma=False,
    )
```

```python
import functools
import math

import jax
import jax.numpy as jnp
import ml_dtypes
import numpy as np
from jax import lax
from jax.experimental import pallas as pl
from jax.experimental.pallas import tpu as pltpu
from jax.sharding import PartitionSpec as P

CYZ = 128
NH = 16
QP = 24
K = 4096
PLANES = 4
SLABS = 16
OWNERS = 32
CELLS = 16
WIDTH = 128
POINTS = QP * QP

section_weights = (0.25, 1.0 / 3.0, 0.5, 1.0)
quad_half = 4.5
fene_limit = 64.0
time_step = 0.005
weight_cube = (2.0 * quad_half / QP) ** 3
code_top = 32600.0
f32 = jnp.float32
bf16 = jnp.bfloat16
MESH = pl.DeviceIdType.MESH

next_owners = [(1, 0), (-1, 0), (0, 1), (1, 1), (-1, 1)]
away_order = (8, 7, -7, 6, -6, 5, -5, 4, -4, 3, -3, 2, -2, 1, -1, 0)
far = [(away, other) for away in away_order[:7] for other in (1, 0)]
near = [(away, other) for away in away_order[7:] for other in (1, 0) if (away, other) != (0, 0)]


def split_table(table):
    high = table.astype(np.float32).astype(ml_dtypes.bfloat16)
    low = (table - high.astype(np.float64)).astype(np.float32).astype(ml_dtypes.bfloat16)
    return np.stack([high, low])


@functools.cache
def tables():
    x = quad_half * (2.0 * np.arange(QP) + 1.0 - QP) / QP
    rows = [np.exp(-0.5 * x * x) * math.pi ** (-0.25)]
    rows.append(math.sqrt(2.0) * x * rows[0])
    for m in range(1, NH - 1):
        rows.append(
            math.sqrt(2.0 / (m + 1.0)) * x * rows[m] - math.sqrt(m / (m + 1.0)) * rows[m - 1]
        )
    h = np.stack(rows)
    inner = np.kron(h, h)
    outer = np.kron(h.T, np.eye(CELLS))
    xb = np.repeat(x, QP)
    xd = np.tile(x, QP)
    square = x[:, None] ** 2 + (xb**2 + xd**2)[None, :]
    ratio = time_step / (1.0 - square / fene_limit)
    zero = np.zeros(POINTS)
    one = np.ones(POINTS)
    moments = np.zeros((3, 16, POINTS))
    moments[0, [4, 5, 7, 8]] = [xb * xb, xb * xd, xb * xd, xd * xd]
    moments[1, [1, 2, 3, 6]] = [xb, xd, xb, xd]
    moments[2, 0] = one
    points = np.stack([xb, xd, xb * xb, xb * xd, xd * xd, zero, zero, zero])
    return (
        x,
        split_table(outer),
        split_table(inner),
        split_table(np.ascontiguousarray(inner.T)),
        split_table(np.ascontiguousarray(outer.T)),
        ratio.astype(np.float32),
        points.astype(np.float32),
        moments.astype(np.float32),
    )


def halves(value):
    high = value.astype(bf16)
    return high, (value - high.astype(f32)).astype(bf16)


def product(left, right):
    total = None
    for i, a in enumerate(left):
        for j, b in enumerate(right):
            if i + j < 2:
                part = jnp.dot(a, b, preferred_element_type=f32)
                total = part if total is None else total + part
    return total


def encode(low, high):
    top = jnp.max(jnp.maximum(jnp.abs(low), jnp.abs(high)), axis=0, keepdims=True)
    level = jnp.ceil(jnp.log2(jnp.maximum(top, 1e-30)) * 2.0)
    unit = jnp.exp2(level * -0.5) * code_top
    low_code = jnp.round(low * unit).astype(jnp.int32)
    high_code = jnp.round(high * unit).astype(jnp.int32)
    word = jnp.bitwise_or(lax.shift_left(high_code, 16), jnp.bitwise_and(low_code, 0xFFFF))
    return word, level.astype(jnp.int32)


def decode(word, level, factor):
    unit = jnp.exp2(level.astype(f32) * 0.5) * (factor / code_top)
    low = lax.shift_right_arithmetic(lax.shift_left(word, 16), 16).astype(f32) * unit
    high = lax.shift_right_arithmetic(word, 16).astype(f32) * unit
    return low, high


def sum_code(value):
    size = jnp.abs(value)
    code = jnp.round((jnp.log2(jnp.maximum(size, 1e-30)) + 100.0) * 2.0**16).astype(jnp.int32)
    code = jnp.where(size < 1e-30, 0, code)
    return jnp.where(value < 0.0, -code, code)


def sum_value(code):
    size = jnp.exp2(jnp.abs(code).astype(f32) * 2.0**-16 - 100.0)
    size = jnp.where(code == 0, 0.0, size)
    return jnp.where(code < 0, -size, size)


def kernel(
    nodes,
    cot, tst, src, cou_hbm, cod_hbm, strain_hbm,
    outer_hbm, inner_hbm, inner_t_hbm, outer_t_hbm, ratio_hbm, points_hbm, moments_hbm,
    back_recv, out_strain, out_courant,
    gbuf, tbuf, scbuf, sct_buf, code_send, code_recv,
    src_recv, mu_send, mu_recv, back_send,
    cou, cod, strain,
    outer_ref, inner_ref, inner_t_ref, outer_t_ref, ratio_ref, points_ref, moments_ref,
    u_buf, es_buf, square_buf, line_buf, column_buf, strain_buf, courant_buf, courant_out,
    local_sem, halo_send, halo_recv, all_send, all_recv, meet_sem,
):
    me = lax.axis_index("coef")
    slab = lax.axis_index("slab")
    above = lax.rem(slab + 1, SLABS)
    below = lax.rem(slab + SLABS - 1, SLABS)
    my_x, my_z = lax.div(me, 16), lax.rem(me, 16)
    my_half, my_mode = lax.rem(me, 2), lax.div(me, 2)
    own = pl.ds(PLANES, PLANES)

    loads = [
        pltpu.make_async_copy(cot, gbuf, local_sem.at[0]),
        pltpu.make_async_copy(tst, tbuf.at[own], local_sem.at[1]),
        pltpu.make_async_copy(outer_hbm, outer_ref, local_sem.at[2]),
        pltpu.make_async_copy(inner_hbm, inner_ref, local_sem.at[3]),
        pltpu.make_async_copy(inner_t_hbm, inner_t_ref, local_sem.at[4]),
        pltpu.make_async_copy(outer_t_hbm, outer_t_ref, local_sem.at[5]),
        pltpu.make_async_copy(
            src.at[pl.ds(pl.multiple_of(me * CELLS, CELLS), CELLS)],
            src_recv.at[my_half, my_mode],
            local_sem.at[6],
        ),
        pltpu.make_async_copy(cou_hbm, cou, local_sem.at[9]),
        pltpu.make_async_copy(cod_hbm, cod, local_sem.at[10]),
        pltpu.make_async_copy(strain_hbm, strain, local_sem.at[11]),
        pltpu.make_async_copy(ratio_hbm, ratio_ref, local_sem.at[12]),
        pltpu.make_async_copy(points_hbm, points_ref, local_sem.at[13]),
        pltpu.make_async_copy(moments_hbm, moments_ref, local_sem.at[14]),
    ]
    barrier = pltpu.get_barrier_semaphore()

    def owner(away, other):
        return lax.rem(my_x + other, 2) * 16 + lax.rem(my_z + away + 16, 16)

    def signal(sem, away, other):
        pl.semaphore_signal(
            sem, inc=1, device_id={"coef": owner(away, other)}, device_id_type=MESH
        )

    pl.semaphore_signal(barrier, inc=1, device_id={"slab": above}, device_id_type=MESH)
    pl.semaphore_signal(barrier, inc=1, device_id={"slab": below}, device_id_type=MESH)
    for away, other in next_owners:
        signal(barrier, away, other)
    for n in (7, 8, 0, 1, 9, 11):
        loads[n].start()
    loads[7].wait()
    loads[8].wait()
    scbuf[1] = jnp.where(cod[...] == 1, -cou[...], cou[...])
    pl.semaphore_wait(barrier, len(next_owners) + 2)

    def halo_copy(way, kind, part):
        target, place = ((above, 0), (below, 2))[way]
        if kind == 0:
            source, dest, sem = scbuf.at[1], scbuf.at[place], 0
        elif kind == 1:
            rows = pl.ds(pl.multiple_of(part * 32, 32), 32)
            planes = pl.ds(place * PLANES, PLANES)
            source, dest, sem = tst.at[:, rows], tbuf.at[planes, rows], 1 + part
        else:
            source, dest, sem = code_send.at[part], code_recv.at[way, part], 5 + part
        return pltpu.make_async_remote_copy(
            src_ref=source,
            dst_ref=dest,
            send_sem=halo_send.at[way, sem],
            recv_sem=halo_recv.at[way, sem],
            device_id={"slab": target},
            device_id_type=MESH,
        )

    first_part = lax.div(lax.rem(me, 8), 2)
    order = [lax.rem(first_part + n, 4) for n in (0, 1, 3, 2)]
    for way in range(2):
        halo_copy(way, 0, 0).start()
    for way in range(2):
        halo_copy(way, 1, order[0]).start()
    loads[0].wait()
    for step in range(4):
        for p in range(PLANES):
            for n in range(2):
                y = order[step] * 32 + n * 16
                word, level = encode(
                    gbuf[p, pl.ds(pl.multiple_of(y, 8), 8), :],
                    gbuf[p, pl.ds(pl.multiple_of(y + 8, 8), 8), :],
                )
                code_send[order[step], p * 2 + n, 0:8, :] = word
                code_send[order[step], p * 2 + n, 8:9, :] = level
        for way in range(2):
            halo_copy(way, 2, order[step]).start()
        if step < 3:
            for way in range(2):
                halo_copy(way, 1, order[step + 1]).start()
    for n in (6, 2, 3, 4, 5, 10, 12):
        loads[n].start()

    for away, other in next_owners:
        signal(meet_sem.at[0], away, other)
    pl.semaphore_wait(meet_sem.at[0], len(next_owners))
    signal(meet_sem.at[1], 2, 0)
    signal(meet_sem.at[1], -2, 0)
    pl.semaphore_wait(meet_sem.at[1], 2)
    signal(meet_sem.at[2], 4, 0)
    signal(meet_sem.at[2], -4, 0)

    def send_source(away, other):
        dest = owner(away, other)
        pltpu.make_async_remote_copy(
            src_ref=src.at[pl.ds(pl.multiple_of(dest * CELLS, CELLS), CELLS)],
            dst_ref=src_recv.at[my_half, my_mode],
            send_sem=all_send.at[0],
            recv_sem=all_recv.at[0],
            device_id={"coef": dest},
            device_id_type=MESH,
        ).start()


    loads[9].wait()
    loads[11].wait()
    column_buf[...] = jnp.zeros((128, 128), f32)
    column_buf[0:9, 0:16] = strain[...]
    strain_turned = jnp.transpose(column_buf[...])[0:16]
    col = [strain_turned[:, p : p + 1] for p in range(9)]
    pts = [points_ref[n : n + 1] for n in range(5)]
    line_buf[...] = (col[1] + col[3]) * pts[0] + (col[2] + col[6]) * pts[1]
    square_buf[...] = col[4] * pts[2] + (col[5] + col[7]) * pts[3] + col[8] * pts[4]

    loads[1].wait()
    for way in range(2):
        halo_copy(way, 0, 0).wait()
    signed = jnp.concatenate([scbuf[0], scbuf[1], scbuf[2], jnp.zeros((116, 128), f32)], axis=0)
    sct_buf[...] = jnp.transpose(signed)
    ones = jnp.ones((8, WIDTH), bf16)

    def chunk(quarter, n):
        part = quarter * 2 + n
        mu_parts, acc_parts = [], []
        coded = [
            (code_recv.at[way, quarter, p * 2 + n], way * 8 + p)
            for way in range(2)
            for p in range(PLANES)
        ]
        unit = {p: jnp.exp2(ref[8:9, :].astype(f32) * 0.5) * (1.0 / code_top) for ref, p in coded}
        for h in range(2):
            y = pl.multiple_of(part * 16 + h * 8, 8)
            sct = sct_buf[pl.ds(y, 8), :]
            wide = [jnp.broadcast_to(sct[:, p : p + 1], (8, WIDTH)) for p in range(12)]
            upper = [c < 0.0 for c in wide]
            c0 = [jnp.maximum(c, 0.0) for c in wide]
            c1 = [jnp.maximum(-c, 0.0) for c in wide]
            speed = [jnp.abs(c) for c in wide]
            s0 = [
                tbuf[p, pl.ds(pl.multiple_of(part * 16, 16), 16), :].astype(f32)[h * 8 : h * 8 + 8]
                for p in range(12)
            ]
            s = dict(enumerate(s0))
            own_change = []
            for n in range(4):
                edge = {p: s[p + 1] - s[p] for p in range(n, 11 - n)}
                change = {p: jnp.where(upper[p], edge[p], edge[p - 1]) for p in range(n + 1, 11 - n)}
                own_change.append([change[p] for p in range(4, 8)])
                if n < 3:
                    s = {p: s0[p] - section_weights[n] * speed[p] * change[p] for p in change}
            g = {p + 4: gbuf[p, pl.ds(y, 8), :] for p in range(PLANES)}
            for ref, p in coded:
                word = ref[0:8, :]
                if h == 0:
                    word = lax.shift_left(word, 16)
                g[p] = lax.shift_right_arithmetic(word, 16).astype(f32) * unit[p]
            mu = [g[p] for p in range(4, 8)]
            acc = [None] * 4
            for k, n in enumerate((3, 2, 1, 0)):
                for p in range(4):
                    term = section_weights[n] * (g[p + 4] * own_change[n][p])
                    acc[p] = term if acc[p] is None else acc[p] + term
                flow = {p: c1[p] * g[p] + c0[p + 1] * g[p + 1] for p in range(k, 11 - k)}
                g = {p: section_weights[n] * (flow[p] - flow[p - 1]) for p in range(k + 1, 11 - k)}
                mu = [mu[p] + g[p + 4] for p in range(4)]
            mu_parts.append(mu)
            acc_parts.append(acc)
        stack = jnp.concatenate(
            [acc_parts[h][p] for p in range(4) for h in range(2)]
            + [jnp.zeros((WIDTH - 4 * CELLS, WIDTH), f32)],
            axis=0,
        )
        total = None
        for piece in halves(stack):
            term = lax.dot_general(
                ones, piece, (((1,), (1,)), ((), ())), preferred_element_type=f32
            )
            total = term if total is None else total + term
        codes = lax.shift_left(sum_code(total[0:1, :]), 8)
        for p in range(4):
            dest = p * 8 + part
            word, level = encode(mu_parts[0][p], mu_parts[1][p])
            mu_send[dest, 0:8, :] = word
            mu_send[dest, 8:9, :] = jnp.bitwise_or(codes, level + 200)

    def chunks(step, _):
        part = lax.rem(first_part + step + lax.div(step, 2) * (5 - 2 * step), 4)
        for kind in (1, 2):
            for way in range(2):
                halo_copy(way, kind, part).wait()

        def half(n, _):
            chunk(part, n)
            return 0

        lax.fori_loop(0, 2, half, 0)
        return 0

    lax.fori_loop(0, 4, chunks, 0)

    pl.semaphore_wait(meet_sem.at[2], 2)
    for away, other in far + near:
        dest = owner(away, other)
        pltpu.make_async_remote_copy(
            src_ref=mu_send.at[dest],
            dst_ref=mu_recv.at[my_half, my_mode],
            send_sem=all_send.at[1],
            recv_sem=all_recv.at[1],
            device_id={"coef": dest},
            device_id_type=MESH,
        ).start()
    own_mu = pltpu.make_async_copy(mu_send.at[me], mu_recv.at[my_half, my_mode], local_sem.at[7])
    own_mu.start()
    for away, other in far:
        send_source(away, other)
    for away, other in near:
        send_source(away, other)

    def wait_all(ref, sem):
        pltpu.make_async_copy(ref, ref, sem).wait()

    src_31 = src.at[pl.ds(0, (OWNERS - 1) * CELLS)]
    for n in (2, 3, 4, 5, 6, 10, 12):
        loads[n].wait()
    outer = (outer_ref[0], outer_ref[1])
    inner = (inner_ref[0], inner_ref[1])

    wait_all(mu_send.at[pl.ds(0, OWNERS - 1)], all_recv.at[1])
    own_mu.wait()
    mu_high, mu_low = [], []
    for half in range(2):
        high_rows, low_rows = [], []
        for mode in range(NH):
            block = jnp.concatenate(
                decode(
                    mu_recv[half, mode, 0:8, :],
                    jnp.bitwise_and(mu_recv[half, mode, 8:9, :], 255) - 200,
                    weight_cube,
                ),
                axis=0,
            )
            high, low = halves(block)
            high_rows.append(high)
            low_rows.append(low)
        mu_high.append(jnp.concatenate(high_rows, axis=0))
        mu_low.append(jnp.concatenate(low_rows, axis=0))
    mu_cells = (jnp.concatenate(mu_high, axis=1), jnp.concatenate(mu_low, axis=1))
    first = halves(product(outer, mu_cells))
    inner_t = (inner_t_ref[0], inner_t_ref[1])
    outer_t = (outer_t_ref[0], outer_t_ref[1])
    line, square = line_buf[...], square_buf[...]
    back = []
    for block in range(3):
        here = slice(block * 128, block * 128 + 128)
        values = product((first[0][here], first[1][here]), inner)
        u_buf[here, :] = values
        weighted = []
        for n in range(8):
            a = block * 8 + n
            u = values[n * CELLS : n * CELLS + CELLS]
            x = float(nodes[a])
            form = (square + x * (line + x * col[0])) * ratio_ref[a : a + 1, :]
            weighted.append(u + u * form)
        back.append(product(halves(jnp.concatenate(weighted, axis=0)), inner_t))
    adj = product(outer_t, halves(jnp.concatenate(back, axis=0)))
    for mode in range(NH):
        for half in range(2):
            dest = 2 * mode + half
            block = adj[mode * CELLS : mode * CELLS + CELLS, half * WIDTH : half * WIDTH + WIDTH]
            word, level = encode(block[0:8], block[8:16])
            back_send[dest, 0:8, :] = word
            back_send[dest, 8:9, :] = level

    def send_back(step, _):
        z = lax.div(step, 2)
        late = z - 8
        z = jnp.where(z < 8, z, jnp.where(z < 12, 15 - late, late + 4))
        dest = lax.rem(step, 2) * 16 + z

        @pl.when(dest != me)
        def _():
            pltpu.make_async_remote_copy(
                src_ref=back_send.at[dest],
                dst_ref=back_recv.at[me],
                send_sem=all_send.at[3],
                recv_sem=all_recv.at[3],
                device_id={"coef": dest},
                device_id_type=MESH,
            ).start()

        return 0

    lax.fori_loop(0, OWNERS, send_back, 0)
    own_back = pltpu.make_async_copy(back_send.at[me], back_recv.at[me], local_sem.at[8])
    own_back.start()

    total = None
    for half in range(2):
        for mode in range(NH):
            row = sum_value(lax.shift_right_arithmetic(mu_recv[half, mode, 8:9, :], 8))
            total = row if total is None else total + row
    courant_buf[...] = jnp.broadcast_to(total, (8, 128))
    turn = lax.rem(128 - lax.div(me, 8) * CELLS, 128)
    turned = pltpu.roll(courant_buf[...], turn, 1) * (-1.0 / math.sqrt(K))
    courant_out[...] = turned[0:1, 0:CELLS]
    outs = [pltpu.make_async_copy(courant_out, out_courant, local_sem.at[15])]
    outs[0].start()

    wait_all(src_31, all_recv.at[0])
    source = jnp.concatenate(
        [src_recv[0].reshape(256, WIDTH), src_recv[1].reshape(256, WIDTH)], axis=1
    )
    es_buf[...] = product(halves(product(outer, (source,))), inner)
    sums = [None, None, None]
    for a in range(QP):
        here = slice(a * CELLS, a * CELLS + CELLS)
        y = u_buf[here, :] * es_buf[here, :] * ratio_ref[a : a + 1, :]
        x = float(nodes[a])
        for n, term in enumerate((y, x * y, (x * x) * y)):
            sums[n] = term if sums[n] is None else sums[n] + term
    strain_sum = None
    for n in range(3):
        part = lax.dot_general(
            moments_ref[n],
            sums[n],
            (((1,), (1,)), ((), ())),
            precision=lax.Precision.HIGHEST,
            preferred_element_type=f32,
        )
        strain_sum = part if strain_sum is None else strain_sum + part
    strain_buf[...] = strain_sum[0:9, :]
    outs.append(pltpu.make_async_copy(strain_buf, out_strain, local_sem.at[16]))
    outs[1].start()

    own_back.wait()
    for copy in outs:
        copy.wait()
    wait_all(src_31, all_send.at[0])
    wait_all(mu_send.at[pl.ds(0, OWNERS - 1)], all_send.at[1])
    wait_all(back_send.at[pl.ds(0, OWNERS - 1)], all_send.at[3])
    wait_all(back_send.at[pl.ds(0, OWNERS - 1)], all_recv.at[3])


def finish(
    back_hbm, strain_hbm, courant_hbm, out_source, out_strain, out_courant, back, source, sem
):
    small = [
        pltpu.make_async_copy(strain_hbm, out_strain, sem.at[0]),
        pltpu.make_async_copy(courant_hbm, out_courant, sem.at[1]),
    ]
    loads = [
        pltpu.make_async_copy(back_hbm.at[here], back.at[here], sem.at[2 + part])
        for part, here in enumerate(pl.ds(n * 8, 8) for n in range(4))
    ]
    for copy in loads + small:
        copy.start()
    stores = []
    for part in range(4):
        loads[part].wait()
        for n in range(part * 8, part * 8 + 8):
            low, high = decode(back[n, 0:8, :], back[n, 8:9, :], 1.0)
            source[n * CELLS : n * CELLS + 8, :] = low
            source[n * CELLS + 8 : n * CELLS + 16, :] = high
        here = pl.ds(part * 128, 128)
        stores.append(pltpu.make_async_copy(source.at[here], out_source.at[here], sem.at[6 + part]))
        stores[-1].start()
    for copy in small + stores:
        copy.wait()


def body(cotangent, transport_state, source_state, courant, upwind_codes, strain_rate):
    nodes, *constants = tables()
    rows = PLANES * CYZ
    hbm = pl.BlockSpec(memory_space=pltpu.HBM)
    results = pl.pallas_call(
        functools.partial(kernel, nodes),
        out_shape=(
            jax.ShapeDtypeStruct((OWNERS, 9, WIDTH), jnp.int32),
            jax.ShapeDtypeStruct((9, CELLS), f32),
            jax.ShapeDtypeStruct((1, CELLS), f32),
        ),
        in_specs=[hbm] * 13,
        out_specs=[hbm] * 3,
        scratch_shapes=[
            pltpu.VMEM((PLANES, CYZ, WIDTH), f32),
            pltpu.VMEM((3 * PLANES, CYZ, WIDTH), bf16),
            pltpu.VMEM((3, PLANES, CYZ), f32),
            pltpu.VMEM((128, 128), f32),
            pltpu.VMEM((4, 2 * PLANES, 9, WIDTH), jnp.int32),
            pltpu.VMEM((2, 4, 2 * PLANES, 9, WIDTH), jnp.int32),
            pltpu.VMEM((2, NH, CELLS, WIDTH), bf16),
            pltpu.VMEM((OWNERS, 9, WIDTH), jnp.int32),
            pltpu.VMEM((2, NH, 9, WIDTH), jnp.int32),
            pltpu.VMEM((OWNERS, 9, WIDTH), jnp.int32),
            pltpu.VMEM((PLANES, CYZ), f32),
            pltpu.VMEM((PLANES, CYZ), jnp.int32),
            pltpu.VMEM((9, CELLS), f32),
            pltpu.VMEM((2, QP * CELLS, NH * CELLS), bf16),
            pltpu.VMEM((2, NH * NH, POINTS), bf16),
            pltpu.VMEM((2, POINTS, NH * NH), bf16),
            pltpu.VMEM((2, NH * CELLS, QP * CELLS), bf16),
            pltpu.VMEM((QP, POINTS), f32),
            pltpu.VMEM((8, POINTS), f32),
            pltpu.VMEM((3, 16, POINTS), f32),
            pltpu.VMEM((QP * CELLS, POINTS), f32),
            pltpu.VMEM((QP * CELLS, POINTS), f32),
            pltpu.VMEM((CELLS, POINTS), f32),
            pltpu.VMEM((CELLS, POINTS), f32),
            pltpu.VMEM((128, 128), f32),
            pltpu.VMEM((9, CELLS), f32),
            pltpu.VMEM((8, WIDTH), f32),
            pltpu.VMEM((1, CELLS), f32),
            pltpu.SemaphoreType.DMA((17,)),
            pltpu.SemaphoreType.DMA((2, 9)),
            pltpu.SemaphoreType.DMA((2, 9)),
            pltpu.SemaphoreType.DMA((4,)),
            pltpu.SemaphoreType.DMA((4,)),
            pltpu.SemaphoreType.REGULAR((3,)),
        ],
        compiler_params=pltpu.CompilerParams(
            collective_id=0, has_side_effects=True, vmem_limit_bytes=60 * 2**20
        ),
    )(
        cotangent.reshape(PLANES, CYZ, WIDTH),
        transport_state.reshape(PLANES, CYZ, WIDTH),
        source_state,
        courant.reshape(PLANES, CYZ),
        upwind_codes.reshape(PLANES, CYZ),
        strain_rate,
        *[jnp.asarray(table) for table in constants],
    )
    adj_source, adj_strain, adj_courant = pl.pallas_call(
        finish,
        out_shape=(
            jax.ShapeDtypeStruct((rows, WIDTH), f32),
            jax.ShapeDtypeStruct((9, CELLS), f32),
            jax.ShapeDtypeStruct((1, CELLS), f32),
        ),
        in_specs=[hbm] * 3,
        out_specs=[hbm] * 3,
        scratch_shapes=[
            pltpu.VMEM((OWNERS, 9, WIDTH), jnp.int32),
            pltpu.VMEM((rows, WIDTH), f32),
            pltpu.SemaphoreType.DMA((10,)),
        ],
        compiler_params=pltpu.CompilerParams(vmem_limit_bytes=60 * 2**20),
    )(*results)
    return adj_source, adj_strain, adj_courant.reshape(CELLS)


def solution(mesh):
    placed = (
        P("slab", "coef"),
        P("slab", "coef"),
        P("slab", "coef"),
        P("slab"),
        P("slab"),
        P(None, ("slab", "coef")),
    )
    return jax.shard_map(
        body,
        mesh=mesh,
        in_specs=placed,
        out_specs=(P("slab", "coef"), P(None, ("slab", "coef")), P(("slab", "coef"))),
        check_vma=False,
    )
```

```python
import functools
import math

import jax
import jax.numpy as jnp
import ml_dtypes
import numpy as np
from jax import lax
from jax.experimental import pallas as pl
from jax.experimental.pallas import tpu as pltpu
from jax.sharding import PartitionSpec as P

CYZ = 128
NH = 16
QP = 24
K = 4096
PLANES = 4
SLABS = 16
OWNERS = 32
CELLS = 16
WIDTH = 128
POINTS = QP * QP

section_weights = (0.25, 1.0 / 3.0, 0.5, 1.0)
quad_half = 4.5
fene_limit = 64.0
time_step = 0.005
weight_cube = (2.0 * quad_half / QP) ** 3
code_top = 32600.0
f32 = jnp.float32
bf16 = jnp.bfloat16
MESH = pl.DeviceIdType.MESH

next_owners = [(1, 0), (-1, 0), (0, 1), (1, 1), (-1, 1)]
away_order = (8, 7, -7, 6, -6, 5, -5, 4, -4, 3, -3, 2, -2, 1, -1, 0)
far = [(away, other) for away in away_order[:7] for other in (1, 0)]
near = [(away, other) for away in away_order[7:] for other in (1, 0) if (away, other) != (0, 0)]


def split_table(table):
    high = table.astype(np.float32).astype(ml_dtypes.bfloat16)
    low = (table - high.astype(np.float64)).astype(np.float32).astype(ml_dtypes.bfloat16)
    return np.stack([high, low])


@functools.cache
def tables():
    x = quad_half * (2.0 * np.arange(QP) + 1.0 - QP) / QP
    rows = [np.exp(-0.5 * x * x) * math.pi ** (-0.25)]
    rows.append(math.sqrt(2.0) * x * rows[0])
    for m in range(1, NH - 1):
        rows.append(
            math.sqrt(2.0 / (m + 1.0)) * x * rows[m] - math.sqrt(m / (m + 1.0)) * rows[m - 1]
        )
    h = np.stack(rows)
    inner = np.kron(h, h)
    outer = np.kron(h.T, np.eye(CELLS))
    xb = np.repeat(x, QP)
    xd = np.tile(x, QP)
    square = x[:, None] ** 2 + (xb**2 + xd**2)[None, :]
    ratio = time_step / (1.0 - square / fene_limit)
    zero = np.zeros(POINTS)
    one = np.ones(POINTS)
    moments = np.zeros((3, 16, POINTS))
    moments[0, [4, 5, 7, 8]] = [xb * xb, xb * xd, xb * xd, xd * xd]
    moments[1, [1, 2, 3, 6]] = [xb, xd, xb, xd]
    moments[2, 0] = one
    points = np.stack([xb, xd, xb * xb, xb * xd, xd * xd, zero, zero, zero])
    return (
        x,
        split_table(outer),
        split_table(inner),
        split_table(np.ascontiguousarray(inner.T)),
        split_table(np.ascontiguousarray(outer.T)),
        ratio.astype(np.float32),
        points.astype(np.float32),
        moments.astype(np.float32),
    )


def halves(value):
    high = value.astype(bf16)
    return high, (value - high.astype(f32)).astype(bf16)


def product(left, right):
    total = None
    for i, a in enumerate(left):
        for j, b in enumerate(right):
            if i + j < 2:
                part = jnp.dot(a, b, preferred_element_type=f32)
                total = part if total is None else total + part
    return total


def encode(low, high):
    top = jnp.max(jnp.maximum(jnp.abs(low), jnp.abs(high)), axis=0, keepdims=True)
    level = jnp.ceil(jnp.log2(jnp.maximum(top, 1e-30)) * 2.0)
    unit = jnp.exp2(level * -0.5) * code_top
    low_code = jnp.round(low * unit).astype(jnp.int32)
    high_code = jnp.round(high * unit).astype(jnp.int32)
    word = jnp.bitwise_or(lax.shift_left(high_code, 16), jnp.bitwise_and(low_code, 0xFFFF))
    return word, level.astype(jnp.int32)


def decode(word, level, factor):
    unit = jnp.exp2(level.astype(f32) * 0.5) * (factor / code_top)
    low = lax.shift_right_arithmetic(lax.shift_left(word, 16), 16).astype(f32) * unit
    high = lax.shift_right_arithmetic(word, 16).astype(f32) * unit
    return low, high


def sum_code(value):
    size = jnp.abs(value)
    code = jnp.round((jnp.log2(jnp.maximum(size, 1e-30)) + 100.0) * 2.0**16).astype(jnp.int32)
    code = jnp.where(size < 1e-30, 0, code)
    return jnp.where(value < 0.0, -code, code)


def sum_value(code):
    size = jnp.exp2(jnp.abs(code).astype(f32) * 2.0**-16 - 100.0)
    size = jnp.where(code == 0, 0.0, size)
    return jnp.where(code < 0, -size, size)


def kernel(
    nodes,
    cot, tst, src, cou_hbm, cod_hbm, strain_hbm,
    outer_hbm, inner_hbm, inner_t_hbm, outer_t_hbm, ratio_hbm, points_hbm, moments_hbm,
    back_recv, out_strain, out_courant,
    gbuf, tbuf, scbuf, sct_buf, code_send, code_recv,
    src_recv, mu_send, mu_recv, back_send,
    cou, cod, strain,
    outer_ref, inner_ref, inner_t_ref, outer_t_ref, ratio_ref, points_ref, moments_ref,
    u_buf, es_buf, square_buf, line_buf, column_buf, courant_buf,
    local_sem, halo_send, halo_recv, all_send, all_recv, meet_sem,
):
    me = lax.axis_index("coef")
    slab = lax.axis_index("slab")
    above = lax.rem(slab + 1, SLABS)
    below = lax.rem(slab + SLABS - 1, SLABS)
    my_x, my_z = lax.div(me, 16), lax.rem(me, 16)
    my_half, my_mode = lax.rem(me, 2), lax.div(me, 2)
    own = pl.ds(PLANES, PLANES)

    loads = [
        pltpu.make_async_copy(cot, gbuf, local_sem.at[0]),
        pltpu.make_async_copy(tst, tbuf.at[own], local_sem.at[1]),
        pltpu.make_async_copy(outer_hbm, outer_ref, local_sem.at[2]),
        pltpu.make_async_copy(inner_hbm, inner_ref, local_sem.at[3]),
        pltpu.make_async_copy(inner_t_hbm, inner_t_ref, local_sem.at[4]),
        pltpu.make_async_copy(outer_t_hbm, outer_t_ref, local_sem.at[5]),
        pltpu.make_async_copy(
            src.at[pl.ds(pl.multiple_of(me * CELLS, CELLS), CELLS)],
            src_recv.at[my_half, my_mode],
            local_sem.at[6],
        ),
        pltpu.make_async_copy(cou_hbm, cou, local_sem.at[9]),
        pltpu.make_async_copy(cod_hbm, cod, local_sem.at[10]),
        pltpu.make_async_copy(strain_hbm, strain, local_sem.at[11]),
        pltpu.make_async_copy(ratio_hbm, ratio_ref, local_sem.at[12]),
        pltpu.make_async_copy(points_hbm, points_ref, local_sem.at[13]),
        pltpu.make_async_copy(moments_hbm, moments_ref, local_sem.at[14]),
    ]
    barrier = pltpu.get_barrier_semaphore()

    def owner(away, other):
        return lax.rem(my_x + other, 2) * 16 + lax.rem(my_z + away + 16, 16)

    def signal(sem, away, other):
        pl.semaphore_signal(
            sem, inc=1, device_id={"coef": owner(away, other)}, device_id_type=MESH
        )

    pl.semaphore_signal(barrier, inc=1, device_id={"slab": above}, device_id_type=MESH)
    pl.semaphore_signal(barrier, inc=1, device_id={"slab": below}, device_id_type=MESH)
    for away, other in next_owners:
        signal(barrier, away, other)
    for n in (7, 8, 0, 1, 9, 11):
        loads[n].start()
    loads[7].wait()
    loads[8].wait()
    scbuf[1] = jnp.where(cod[...] == 1, -cou[...], cou[...])
    pl.semaphore_wait(barrier, len(next_owners) + 2)

    def halo_copy(way, kind, part):
        target, place = ((above, 0), (below, 2))[way]
        if kind == 0:
            source, dest, sem = scbuf.at[1], scbuf.at[place], 0
        elif kind == 1:
            rows = pl.ds(pl.multiple_of(part * 32, 32), 32)
            planes = pl.ds(place * PLANES, PLANES)
            source, dest, sem = tst.at[:, rows], tbuf.at[planes, rows], 1 + part
        else:
            source, dest, sem = code_send.at[part], code_recv.at[way, part], 5 + part
        return pltpu.make_async_remote_copy(
            src_ref=source,
            dst_ref=dest,
            send_sem=halo_send.at[way, sem],
            recv_sem=halo_recv.at[way, sem],
            device_id={"slab": target},
            device_id_type=MESH,
        )

    first_part = lax.div(lax.rem(me, 8), 2)
    order = [lax.rem(first_part + n, 4) for n in (0, 1, 3, 2)]
    for way in range(2):
        halo_copy(way, 0, 0).start()
    for way in range(2):
        halo_copy(way, 1, order[0]).start()
    loads[0].wait()
    for step in range(4):
        for p in range(PLANES):
            for n in range(2):
                y = order[step] * 32 + n * 16
                word, level = encode(
                    gbuf[p, pl.ds(pl.multiple_of(y, 8), 8), :],
                    gbuf[p, pl.ds(pl.multiple_of(y + 8, 8), 8), :],
                )
                code_send[order[step], p * 2 + n, 0:8, :] = word
                code_send[order[step], p * 2 + n, 8:9, :] = level
        for way in range(2):
            halo_copy(way, 2, order[step]).start()
        if step < 3:
            for way in range(2):
                halo_copy(way, 1, order[step + 1]).start()
    for n in (6, 2, 3, 4, 5, 10, 12):
        loads[n].start()

    for away, other in next_owners:
        signal(meet_sem.at[0], away, other)
    pl.semaphore_wait(meet_sem.at[0], len(next_owners))
    signal(meet_sem.at[1], 2, 0)
    signal(meet_sem.at[1], -2, 0)
    pl.semaphore_wait(meet_sem.at[1], 2)
    signal(meet_sem.at[2], 4, 0)
    signal(meet_sem.at[2], -4, 0)

    def send_source(away, other):
        dest = owner(away, other)
        pltpu.make_async_remote_copy(
            src_ref=src.at[pl.ds(pl.multiple_of(dest * CELLS, CELLS), CELLS)],
            dst_ref=src_recv.at[my_half, my_mode],
            send_sem=all_send.at[0],
            recv_sem=all_recv.at[0],
            device_id={"coef": dest},
            device_id_type=MESH,
        ).start()


    loads[9].wait()
    loads[11].wait()
    column_buf[...] = jnp.zeros((128, 128), f32)
    column_buf[0:9, 0:16] = strain[...]
    strain_turned = jnp.transpose(column_buf[...])[0:16]
    col = [strain_turned[:, p : p + 1] for p in range(9)]
    pts = [points_ref[n : n + 1] for n in range(5)]
    line_buf[...] = (col[1] + col[3]) * pts[0] + (col[2] + col[6]) * pts[1]
    square_buf[...] = col[4] * pts[2] + (col[5] + col[7]) * pts[3] + col[8] * pts[4]

    loads[1].wait()
    for way in range(2):
        halo_copy(way, 0, 0).wait()
    signed = jnp.concatenate([scbuf[0], scbuf[1], scbuf[2], jnp.zeros((116, 128), f32)], axis=0)
    sct_buf[...] = jnp.transpose(signed)
    ones = jnp.ones((8, WIDTH), bf16)

    def chunk(quarter, n):
        part = quarter * 2 + n
        mu_parts, acc_parts = [], []
        coded = [
            (code_recv.at[way, quarter, p * 2 + n], way * 8 + p)
            for way in range(2)
            for p in range(PLANES)
        ]
        unit = {p: jnp.exp2(ref[8:9, :].astype(f32) * 0.5) * (1.0 / code_top) for ref, p in coded}
        for h in range(2):
            y = pl.multiple_of(part * 16 + h * 8, 8)
            sct = sct_buf[pl.ds(y, 8), :]
            wide = [jnp.broadcast_to(sct[:, p : p + 1], (8, WIDTH)) for p in range(12)]
            upper = [c < 0.0 for c in wide]
            c0 = [jnp.maximum(c, 0.0) for c in wide]
            c1 = [jnp.maximum(-c, 0.0) for c in wide]
            speed = [jnp.abs(c) for c in wide]
            s0 = [
                tbuf[p, pl.ds(pl.multiple_of(part * 16, 16), 16), :].astype(f32)[h * 8 : h * 8 + 8]
                for p in range(12)
            ]
            s = dict(enumerate(s0))
            own_change = []
            for n in range(4):
                edge = {p: s[p + 1] - s[p] for p in range(n, 11 - n)}
                change = {p: jnp.where(upper[p], edge[p], edge[p - 1]) for p in range(n + 1, 11 - n)}
                own_change.append([change[p] for p in range(4, 8)])
                if n < 3:
                    s = {p: s0[p] - section_weights[n] * speed[p] * change[p] for p in change}
            g = {p + 4: gbuf[p, pl.ds(y, 8), :] for p in range(PLANES)}
            for ref, p in coded:
                word = ref[0:8, :]
                if h == 0:
                    word = lax.shift_left(word, 16)
                g[p] = lax.shift_right_arithmetic(word, 16).astype(f32) * unit[p]
            mu = [g[p] for p in range(4, 8)]
            acc = [None] * 4
            for k, n in enumerate((3, 2, 1, 0)):
                for p in range(4):
                    term = section_weights[n] * (g[p + 4] * own_change[n][p])
                    acc[p] = term if acc[p] is None else acc[p] + term
                flow = {p: c1[p] * g[p] + c0[p + 1] * g[p + 1] for p in range(k, 11 - k)}
                g = {p: section_weights[n] * (flow[p] - flow[p - 1]) for p in range(k + 1, 11 - k)}
                mu = [mu[p] + g[p + 4] for p in range(4)]
            mu_parts.append(mu)
            acc_parts.append(acc)
        stack = jnp.concatenate(
            [acc_parts[h][p] for p in range(4) for h in range(2)]
            + [jnp.zeros((WIDTH - 4 * CELLS, WIDTH), f32)],
            axis=0,
        )
        total = None
        for piece in halves(stack):
            term = lax.dot_general(
                ones, piece, (((1,), (1,)), ((), ())), preferred_element_type=f32
            )
            total = term if total is None else total + term
        codes = lax.shift_left(sum_code(total[0:1, :]), 8)
        for p in range(4):
            dest = p * 8 + part
            word, level = encode(mu_parts[0][p], mu_parts[1][p])
            mu_send[dest, 0:8, :] = word
            mu_send[dest, 8:9, :] = jnp.bitwise_or(codes, level + 200)

    def chunks(step, _):
        part = lax.rem(first_part + step + lax.div(step, 2) * (5 - 2 * step), 4)
        for kind in (1, 2):
            for way in range(2):
                halo_copy(way, kind, part).wait()

        def half(n, _):
            chunk(part, n)
            return 0

        lax.fori_loop(0, 2, half, 0)
        return 0

    lax.fori_loop(0, 4, chunks, 0)

    pl.semaphore_wait(meet_sem.at[2], 2)
    for away, other in far + near:
        dest = owner(away, other)
        pltpu.make_async_remote_copy(
            src_ref=mu_send.at[dest],
            dst_ref=mu_recv.at[my_half, my_mode],
            send_sem=all_send.at[1],
            recv_sem=all_recv.at[1],
            device_id={"coef": dest},
            device_id_type=MESH,
        ).start()
    own_mu = pltpu.make_async_copy(mu_send.at[me], mu_recv.at[my_half, my_mode], local_sem.at[7])
    own_mu.start()
    for away, other in far:
        send_source(away, other)
    for away, other in near:
        send_source(away, other)

    def wait_all(ref, sem):
        pltpu.make_async_copy(ref, ref, sem).wait()

    src_31 = src.at[pl.ds(0, (OWNERS - 1) * CELLS)]
    for n in (2, 3, 4, 5, 6, 10, 12):
        loads[n].wait()
    outer = (outer_ref[0], outer_ref[1])
    inner = (inner_ref[0], inner_ref[1])

    wait_all(mu_send.at[pl.ds(0, OWNERS - 1)], all_recv.at[1])
    own_mu.wait()
    mu_high, mu_low = [], []
    for half in range(2):
        high_rows, low_rows = [], []
        for mode in range(NH):
            block = jnp.concatenate(
                decode(
                    mu_recv[half, mode, 0:8, :],
                    jnp.bitwise_and(mu_recv[half, mode, 8:9, :], 255) - 200,
                    weight_cube,
                ),
                axis=0,
            )
            high, low = halves(block)
            high_rows.append(high)
            low_rows.append(low)
        mu_high.append(jnp.concatenate(high_rows, axis=0))
        mu_low.append(jnp.concatenate(low_rows, axis=0))
    mu_cells = (jnp.concatenate(mu_high, axis=1), jnp.concatenate(mu_low, axis=1))
    first = halves(product(outer, mu_cells))
    inner_t = (inner_t_ref[0], inner_t_ref[1])
    outer_t = (outer_t_ref[0], outer_t_ref[1])
    line, square = line_buf[...], square_buf[...]
    back = []
    for block in range(3):
        here = slice(block * 128, block * 128 + 128)
        values = product((first[0][here], first[1][here]), inner)
        u_buf[here, :] = values
        weighted = []
        for n in range(8):
            a = block * 8 + n
            u = values[n * CELLS : n * CELLS + CELLS]
            x = float(nodes[a])
            form = (square + x * (line + x * col[0])) * ratio_ref[a : a + 1, :]
            weighted.append(u + u * form)
        back.append(product(halves(jnp.concatenate(weighted, axis=0)), inner_t))
    adj = product(outer_t, halves(jnp.concatenate(back, axis=0)))
    for mode in range(NH):
        for half in range(2):
            dest = 2 * mode + half
            block = adj[mode * CELLS : mode * CELLS + CELLS, half * WIDTH : half * WIDTH + WIDTH]
            word, level = encode(block[0:8], block[8:16])
            back_send[dest, 0:8, :] = word
            back_send[dest, 8:9, :] = level

    def send_back(step, _):
        z = lax.div(step, 2)
        late = z - 8
        z = jnp.where(z < 8, z, jnp.where(z < 12, 15 - late, late + 4))
        dest = lax.rem(step, 2) * 16 + z

        @pl.when(dest != me)
        def _():
            pltpu.make_async_remote_copy(
                src_ref=back_send.at[dest],
                dst_ref=back_recv.at[me],
                send_sem=all_send.at[3],
                recv_sem=all_recv.at[3],
                device_id={"coef": dest},
                device_id_type=MESH,
            ).start()

        return 0

    lax.fori_loop(0, OWNERS, send_back, 0)
    own_back = pltpu.make_async_copy(back_send.at[me], back_recv.at[me], local_sem.at[8])
    own_back.start()

    total = None
    for half in range(2):
        for mode in range(NH):
            row = sum_value(lax.shift_right_arithmetic(mu_recv[half, mode, 8:9, :], 8))
            total = row if total is None else total + row
    courant_buf[...] = jnp.broadcast_to(total, (8, 128))
    turn = lax.rem(128 - lax.div(me, 8) * CELLS, 128)
    turned = pltpu.roll(courant_buf[...], turn, 1) * (-1.0 / math.sqrt(K))
    out_courant[...] = turned[0:1, 0:CELLS]

    wait_all(src_31, all_recv.at[0])
    source = jnp.concatenate(
        [src_recv[0].reshape(256, WIDTH), src_recv[1].reshape(256, WIDTH)], axis=1
    )
    es_buf[...] = product(halves(product(outer, (source,))), inner)
    sums = [None, None, None]
    for a in range(QP):
        here = slice(a * CELLS, a * CELLS + CELLS)
        y = u_buf[here, :] * es_buf[here, :] * ratio_ref[a : a + 1, :]
        x = float(nodes[a])
        for n, term in enumerate((y, x * y, (x * x) * y)):
            sums[n] = term if sums[n] is None else sums[n] + term
    strain_sum = None
    for n in range(3):
        part = lax.dot_general(
            moments_ref[n],
            sums[n],
            (((1,), (1,)), ((), ())),
            precision=lax.Precision.HIGHEST,
            preferred_element_type=f32,
        )
        strain_sum = part if strain_sum is None else strain_sum + part
    out_strain[...] = strain_sum[0:9, :]

    own_back.wait()
    wait_all(src_31, all_send.at[0])
    wait_all(mu_send.at[pl.ds(0, OWNERS - 1)], all_send.at[1])
    wait_all(back_send.at[pl.ds(0, OWNERS - 1)], all_send.at[3])
    wait_all(back_send.at[pl.ds(0, OWNERS - 1)], all_recv.at[3])


def finish(back, strain, courant, out_source, out_strain, out_courant, source, sem):
    stores = [
        pltpu.make_async_copy(strain, out_strain, sem.at[0]),
        pltpu.make_async_copy(courant, out_courant, sem.at[1]),
    ]
    for copy in stores:
        copy.start()
    for part in range(4):
        for n in range(part * 8, part * 8 + 8):
            low, high = decode(back[n, 0:8, :], back[n, 8:9, :], 1.0)
            source[n * CELLS : n * CELLS + 8, :] = low
            source[n * CELLS + 8 : n * CELLS + 16, :] = high
        here = pl.ds(part * 128, 128)
        stores.append(pltpu.make_async_copy(source.at[here], out_source.at[here], sem.at[2 + part]))
        stores[-1].start()
    for copy in stores:
        copy.wait()


def body(cotangent, transport_state, source_state, courant, upwind_codes, strain_rate):
    nodes, *constants = tables()
    rows = PLANES * CYZ
    hbm = pl.BlockSpec(memory_space=pltpu.HBM)
    vmem = pl.BlockSpec(memory_space=pltpu.VMEM)
    results = pl.pallas_call(
        functools.partial(kernel, nodes),
        out_shape=(
            jax.ShapeDtypeStruct((OWNERS, 9, WIDTH), jnp.int32),
            jax.ShapeDtypeStruct((9, CELLS), f32),
            jax.ShapeDtypeStruct((1, CELLS), f32),
        ),
        in_specs=[hbm] * 13,
        out_specs=[vmem] * 3,
        scratch_shapes=[
            pltpu.VMEM((PLANES, CYZ, WIDTH), f32),
            pltpu.VMEM((3 * PLANES, CYZ, WIDTH), bf16),
            pltpu.VMEM((3, PLANES, CYZ), f32),
            pltpu.VMEM((128, 128), f32),
            pltpu.VMEM((4, 2 * PLANES, 9, WIDTH), jnp.int32),
            pltpu.VMEM((2, 4, 2 * PLANES, 9, WIDTH), jnp.int32),
            pltpu.VMEM((2, NH, CELLS, WIDTH), bf16),
            pltpu.VMEM((OWNERS, 9, WIDTH), jnp.int32),
            pltpu.VMEM((2, NH, 9, WIDTH), jnp.int32),
            pltpu.VMEM((OWNERS, 9, WIDTH), jnp.int32),
            pltpu.VMEM((PLANES, CYZ), f32),
            pltpu.VMEM((PLANES, CYZ), jnp.int32),
            pltpu.VMEM((9, CELLS), f32),
            pltpu.VMEM((2, QP * CELLS, NH * CELLS), bf16),
            pltpu.VMEM((2, NH * NH, POINTS), bf16),
            pltpu.VMEM((2, POINTS, NH * NH), bf16),
            pltpu.VMEM((2, NH * CELLS, QP * CELLS), bf16),
            pltpu.VMEM((QP, POINTS), f32),
            pltpu.VMEM((8, POINTS), f32),
            pltpu.VMEM((3, 16, POINTS), f32),
            pltpu.VMEM((QP * CELLS, POINTS), f32),
            pltpu.VMEM((QP * CELLS, POINTS), f32),
            pltpu.VMEM((CELLS, POINTS), f32),
            pltpu.VMEM((CELLS, POINTS), f32),
            pltpu.VMEM((128, 128), f32),
            pltpu.VMEM((8, WIDTH), f32),
            pltpu.SemaphoreType.DMA((15,)),
            pltpu.SemaphoreType.DMA((2, 9)),
            pltpu.SemaphoreType.DMA((2, 9)),
            pltpu.SemaphoreType.DMA((4,)),
            pltpu.SemaphoreType.DMA((4,)),
            pltpu.SemaphoreType.REGULAR((3,)),
        ],
        compiler_params=pltpu.CompilerParams(
            collective_id=0, has_side_effects=True, vmem_limit_bytes=30 * 2**20
        ),
    )(
        *[
            pltpu.with_memory_space_constraint(array, pltpu.HBM)
            for array in (
                cotangent.reshape(PLANES, CYZ, WIDTH),
                transport_state.reshape(PLANES, CYZ, WIDTH),
                source_state,
                courant.reshape(PLANES, CYZ),
                upwind_codes.reshape(PLANES, CYZ),
                strain_rate,
                *[jnp.asarray(table) for table in constants],
            )
        ],
    )
    adj_source, adj_strain, adj_courant = pl.pallas_call(
        finish,
        out_shape=(
            jax.ShapeDtypeStruct((rows, WIDTH), f32),
            jax.ShapeDtypeStruct((9, CELLS), f32),
            jax.ShapeDtypeStruct((1, CELLS), f32),
        ),
        in_specs=[vmem] * 3,
        out_specs=[hbm] * 3,
        scratch_shapes=[
            pltpu.VMEM((rows, WIDTH), f32),
            pltpu.SemaphoreType.DMA((6,)),
        ],
        compiler_params=pltpu.CompilerParams(vmem_limit_bytes=8 * 2**20),
    )(*results)
    return adj_source, adj_strain, adj_courant.reshape(CELLS)


def solution(mesh):
    placed = (
        P("slab", "coef"),
        P("slab", "coef"),
        P("slab", "coef"),
        P("slab"),
        P("slab"),
        P(None, ("slab", "coef")),
    )
    return jax.shard_map(
        body,
        mesh=mesh,
        in_specs=placed,
        out_specs=(P("slab", "coef"), P(None, ("slab", "coef")), P(("slab", "coef"))),
        check_vma=False,
    )
```

```python
import functools
import math

import jax
import jax.numpy as jnp
import ml_dtypes
import numpy as np
from jax import lax
from jax.experimental import pallas as pl
from jax.experimental.pallas import tpu as pltpu
from jax.sharding import PartitionSpec as P

CYZ = 128
NH = 16
QP = 24
K = 4096
PLANES = 4
SLABS = 16
OWNERS = 32
CELLS = 16
WIDTH = 128
POINTS = QP * QP

section_weights = (0.25, 1.0 / 3.0, 0.5, 1.0)
quad_half = 4.5
fene_limit = 64.0
time_step = 0.005
weight_cube = (2.0 * quad_half / QP) ** 3
code_top = 32600.0
f32 = jnp.float32
bf16 = jnp.bfloat16
MESH = pl.DeviceIdType.MESH

next_owners = [(1, 0), (-1, 0), (0, 1), (1, 1), (-1, 1)]
away_order = (8, 7, -7, 6, -6, 5, -5, 4, -4, 3, -3, 2, -2, 1, -1, 0)
far = [(away, other) for away in away_order[:7] for other in (1, 0)]
near = [(away, other) for away in away_order[7:] for other in (1, 0) if (away, other) != (0, 0)]


def split_table(table):
    high = table.astype(np.float32).astype(ml_dtypes.bfloat16)
    low = (table - high.astype(np.float64)).astype(np.float32).astype(ml_dtypes.bfloat16)
    return np.stack([high, low])


@functools.cache
def tables():
    x = quad_half * (2.0 * np.arange(QP) + 1.0 - QP) / QP
    rows = [np.exp(-0.5 * x * x) * math.pi ** (-0.25)]
    rows.append(math.sqrt(2.0) * x * rows[0])
    for m in range(1, NH - 1):
        rows.append(
            math.sqrt(2.0 / (m + 1.0)) * x * rows[m] - math.sqrt(m / (m + 1.0)) * rows[m - 1]
        )
    h = np.stack(rows)
    inner = np.kron(h, h)
    outer = np.kron(h.T, np.eye(CELLS))
    xb = np.repeat(x, QP)
    xd = np.tile(x, QP)
    square = x[:, None] ** 2 + (xb**2 + xd**2)[None, :]
    ratio = time_step / (1.0 - square / fene_limit)
    zero = np.zeros(POINTS)
    one = np.ones(POINTS)
    moments = np.zeros((3, 16, POINTS))
    moments[0, [4, 5, 7, 8]] = [xb * xb, xb * xd, xb * xd, xd * xd]
    moments[1, [1, 2, 3, 6]] = [xb, xd, xb, xd]
    moments[2, 0] = one
    points = np.stack([xb, xd, xb * xb, xb * xd, xd * xd, zero, zero, zero])
    return (
        x,
        split_table(outer),
        split_table(inner),
        split_table(np.ascontiguousarray(inner.T)),
        split_table(np.ascontiguousarray(outer.T)),
        ratio.astype(np.float32),
        points.astype(np.float32),
        moments.astype(np.float32),
    )


def halves(value):
    high = value.astype(bf16)
    return high, (value - high.astype(f32)).astype(bf16)


def product(left, right):
    total = None
    for i, a in enumerate(left):
        for j, b in enumerate(right):
            if i + j < 2:
                part = jnp.dot(a, b, preferred_element_type=f32)
                total = part if total is None else total + part
    return total


def encode(low, high):
    top = jnp.max(jnp.maximum(jnp.abs(low), jnp.abs(high)), axis=0, keepdims=True)
    level = jnp.ceil(jnp.log2(jnp.maximum(top, 1e-30)) * 2.0)
    unit = jnp.exp2(level * -0.5) * code_top
    low_code = jnp.round(low * unit).astype(jnp.int32)
    high_code = jnp.round(high * unit).astype(jnp.int32)
    word = jnp.bitwise_or(lax.shift_left(high_code, 16), jnp.bitwise_and(low_code, 0xFFFF))
    return word, level.astype(jnp.int32)


def decode(word, level, factor):
    unit = jnp.exp2(level.astype(f32) * 0.5) * (factor / code_top)
    low = lax.shift_right_arithmetic(lax.shift_left(word, 16), 16).astype(f32) * unit
    high = lax.shift_right_arithmetic(word, 16).astype(f32) * unit
    return low, high


def sum_code(value):
    size = jnp.abs(value)
    code = jnp.round((jnp.log2(jnp.maximum(size, 1e-30)) + 100.0) * 2.0**16).astype(jnp.int32)
    code = jnp.where(size < 1e-30, 0, code)
    return jnp.where(value < 0.0, -code, code)


def sum_value(code):
    size = jnp.exp2(jnp.abs(code).astype(f32) * 2.0**-16 - 100.0)
    size = jnp.where(code == 0, 0.0, size)
    return jnp.where(code < 0, -size, size)


def kernel(
    nodes,
    cot, tst, src, cou_hbm, cod_hbm, strain_hbm,
    outer_hbm, inner_hbm, inner_t_hbm, outer_t_hbm, ratio_hbm, points_hbm, moments_hbm,
    back_recv, out_strain, out_courant,
    gbuf, tbuf, scbuf, sct_buf, code_send, code_recv,
    src_recv, mu_send, mu_recv, back_send,
    cou, cod, strain,
    outer_ref, inner_ref, inner_t_ref, outer_t_ref, ratio_ref, points_ref, moments_ref,
    u_buf, es_buf, square_buf, line_buf, column_buf, courant_buf,
    local_sem, halo_send, halo_recv, all_send, all_recv, meet_sem,
):
    me = lax.axis_index("coef")
    slab = lax.axis_index("slab")
    above = lax.rem(slab + 1, SLABS)
    below = lax.rem(slab + SLABS - 1, SLABS)
    my_x, my_z = lax.div(me, 16), lax.rem(me, 16)
    my_half, my_mode = lax.rem(me, 2), lax.div(me, 2)
    own = pl.ds(PLANES, PLANES)

    loads = [
        pltpu.make_async_copy(cot, gbuf, local_sem.at[0]),
        pltpu.make_async_copy(tst, tbuf.at[own], local_sem.at[1]),
        pltpu.make_async_copy(outer_hbm, outer_ref, local_sem.at[2]),
        pltpu.make_async_copy(inner_hbm, inner_ref, local_sem.at[3]),
        pltpu.make_async_copy(inner_t_hbm, inner_t_ref, local_sem.at[4]),
        pltpu.make_async_copy(outer_t_hbm, outer_t_ref, local_sem.at[5]),
        pltpu.make_async_copy(
            src.at[pl.ds(pl.multiple_of(me * CELLS, CELLS), CELLS)],
            src_recv.at[my_half, my_mode],
            local_sem.at[6],
        ),
        pltpu.make_async_copy(cou_hbm, cou, local_sem.at[9]),
        pltpu.make_async_copy(cod_hbm, cod, local_sem.at[10]),
        pltpu.make_async_copy(strain_hbm, strain, local_sem.at[11]),
        pltpu.make_async_copy(ratio_hbm, ratio_ref, local_sem.at[12]),
        pltpu.make_async_copy(points_hbm, points_ref, local_sem.at[13]),
        pltpu.make_async_copy(moments_hbm, moments_ref, local_sem.at[14]),
    ]
    barrier = pltpu.get_barrier_semaphore()

    def owner(away, other):
        return lax.rem(my_x + other, 2) * 16 + lax.rem(my_z + away + 16, 16)

    def signal(sem, away, other):
        pl.semaphore_signal(
            sem, inc=1, device_id={"coef": owner(away, other)}, device_id_type=MESH
        )

    pl.semaphore_signal(barrier, inc=1, device_id={"slab": above}, device_id_type=MESH)
    pl.semaphore_signal(barrier, inc=1, device_id={"slab": below}, device_id_type=MESH)
    for away, other in next_owners:
        signal(barrier, away, other)
    for n in (7, 8, 0, 1, 9, 11):
        loads[n].start()
    loads[7].wait()
    loads[8].wait()
    scbuf[1] = jnp.where(cod[...] == 1, -cou[...], cou[...])
    pl.semaphore_wait(barrier, len(next_owners) + 2)

    def halo_copy(way, kind, part):
        target, place = ((above, 0), (below, 2))[way]
        if kind == 0:
            source, dest, sem = scbuf.at[1], scbuf.at[place], 0
        elif kind == 1:
            rows = pl.ds(pl.multiple_of(part * 16, 16), 16)
            planes = pl.ds(place * PLANES, PLANES)
            source, dest, sem = tst.at[:, rows], tbuf.at[planes, rows], 1 + part
        else:
            source, dest, sem = code_send.at[part], code_recv.at[way, part], 9 + part
        return pltpu.make_async_remote_copy(
            src_ref=source,
            dst_ref=dest,
            send_sem=halo_send.at[way, sem],
            recv_sem=halo_recv.at[way, sem],
            device_id={"slab": target},
            device_id_type=MESH,
        )

    first_part = lax.rem(me, 8)
    order = [lax.rem(first_part + n, 8) for n in range(8)]
    for way in range(2):
        halo_copy(way, 0, 0).start()
    for way in range(2):
        halo_copy(way, 1, order[0]).start()
    loads[0].wait()
    for step in range(8):
        for p in range(PLANES):
            y = order[step] * 16
            word, level = encode(
                gbuf[p, pl.ds(pl.multiple_of(y, 8), 8), :],
                gbuf[p, pl.ds(pl.multiple_of(y + 8, 8), 8), :],
            )
            code_send[order[step], p, 0:8, :] = word
            code_send[order[step], p, 8:9, :] = level
        for way in range(2):
            halo_copy(way, 2, order[step]).start()
        if step < 7:
            for way in range(2):
                halo_copy(way, 1, order[step + 1]).start()
    for n in (6, 2, 3, 4, 5, 10, 12):
        loads[n].start()

    for away, other in next_owners:
        signal(meet_sem.at[0], away, other)
    pl.semaphore_wait(meet_sem.at[0], len(next_owners))
    signal(meet_sem.at[1], 2, 0)
    signal(meet_sem.at[1], -2, 0)
    pl.semaphore_wait(meet_sem.at[1], 2)
    signal(meet_sem.at[2], 4, 0)
    signal(meet_sem.at[2], -4, 0)

    def send_source(away, other):
        dest = owner(away, other)
        pltpu.make_async_remote_copy(
            src_ref=src.at[pl.ds(pl.multiple_of(dest * CELLS, CELLS), CELLS)],
            dst_ref=src_recv.at[my_half, my_mode],
            send_sem=all_send.at[0],
            recv_sem=all_recv.at[0],
            device_id={"coef": dest},
            device_id_type=MESH,
        ).start()


    loads[9].wait()
    loads[11].wait()
    column_buf[...] = jnp.zeros((128, 128), f32)
    column_buf[0:9, 0:16] = strain[...]
    strain_turned = jnp.transpose(column_buf[...])[0:16]
    col = [strain_turned[:, p : p + 1] for p in range(9)]
    pts = [points_ref[n : n + 1] for n in range(5)]
    line_buf[...] = (col[1] + col[3]) * pts[0] + (col[2] + col[6]) * pts[1]
    square_buf[...] = col[4] * pts[2] + (col[5] + col[7]) * pts[3] + col[8] * pts[4]

    loads[1].wait()
    for way in range(2):
        halo_copy(way, 0, 0).wait()
    signed = jnp.concatenate([scbuf[0], scbuf[1], scbuf[2], jnp.zeros((116, 128), f32)], axis=0)
    sct_buf[...] = jnp.transpose(signed)
    ones = jnp.ones((8, WIDTH), bf16)

    def chunk(part):
        mu_parts, acc_parts = [], []
        coded = [
            (code_recv.at[way, part, p], way * 8 + p)
            for way in range(2)
            for p in range(PLANES)
        ]
        unit = {p: jnp.exp2(ref[8:9, :].astype(f32) * 0.5) * (1.0 / code_top) for ref, p in coded}
        for h in range(2):
            y = pl.multiple_of(part * 16 + h * 8, 8)
            sct = sct_buf[pl.ds(y, 8), :]
            wide = [jnp.broadcast_to(sct[:, p : p + 1], (8, WIDTH)) for p in range(12)]
            upper = [c < 0.0 for c in wide]
            c0 = [jnp.maximum(c, 0.0) for c in wide]
            c1 = [jnp.maximum(-c, 0.0) for c in wide]
            speed = [jnp.abs(c) for c in wide]
            s0 = [
                tbuf[p, pl.ds(pl.multiple_of(part * 16, 16), 16), :].astype(f32)[h * 8 : h * 8 + 8]
                for p in range(12)
            ]
            s = dict(enumerate(s0))
            own_change = []
            for n in range(4):
                edge = {p: s[p + 1] - s[p] for p in range(n, 11 - n)}
                change = {p: jnp.where(upper[p], edge[p], edge[p - 1]) for p in range(n + 1, 11 - n)}
                own_change.append([change[p] for p in range(4, 8)])
                if n < 3:
                    s = {p: s0[p] - section_weights[n] * speed[p] * change[p] for p in change}
            g = {p + 4: gbuf[p, pl.ds(y, 8), :] for p in range(PLANES)}
            for ref, p in coded:
                word = ref[0:8, :]
                if h == 0:
                    word = lax.shift_left(word, 16)
                g[p] = lax.shift_right_arithmetic(word, 16).astype(f32) * unit[p]
            mu = [g[p] for p in range(4, 8)]
            acc = [None] * 4
            for k, n in enumerate((3, 2, 1, 0)):
                for p in range(4):
                    term = section_weights[n] * (g[p + 4] * own_change[n][p])
                    acc[p] = term if acc[p] is None else acc[p] + term
                flow = {p: c1[p] * g[p] + c0[p + 1] * g[p + 1] for p in range(k, 11 - k)}
                g = {p: section_weights[n] * (flow[p] - flow[p - 1]) for p in range(k + 1, 11 - k)}
                mu = [mu[p] + g[p + 4] for p in range(4)]
            mu_parts.append(mu)
            acc_parts.append(acc)
        stack = jnp.concatenate(
            [acc_parts[h][p] for p in range(4) for h in range(2)]
            + [jnp.zeros((WIDTH - 4 * CELLS, WIDTH), f32)],
            axis=0,
        )
        total = None
        for piece in halves(stack):
            term = lax.dot_general(
                ones, piece, (((1,), (1,)), ((), ())), preferred_element_type=f32
            )
            total = term if total is None else total + term
        codes = lax.shift_left(sum_code(total[0:1, :]), 8)
        for p in range(4):
            dest = p * 8 + part
            word, level = encode(mu_parts[0][p], mu_parts[1][p])
            mu_send[dest, 0:8, :] = word
            mu_send[dest, 8:9, :] = jnp.bitwise_or(codes, level + 200)

    def chunks(step, _):
        part = lax.rem(first_part + step, 8)
        for kind in (1, 2):
            for way in range(2):
                halo_copy(way, kind, part).wait()

        chunk(part)
        return 0

    lax.fori_loop(0, 8, chunks, 0)

    pl.semaphore_wait(meet_sem.at[2], 2)
    for away, other in far + near:
        dest = owner(away, other)
        pltpu.make_async_remote_copy(
            src_ref=mu_send.at[dest],
            dst_ref=mu_recv.at[my_half, my_mode],
            send_sem=all_send.at[1],
            recv_sem=all_recv.at[1],
            device_id={"coef": dest},
            device_id_type=MESH,
        ).start()
    own_mu = pltpu.make_async_copy(mu_send.at[me], mu_recv.at[my_half, my_mode], local_sem.at[7])
    own_mu.start()
    for away, other in far:
        send_source(away, other)
    for away, other in near:
        send_source(away, other)

    def wait_all(ref, sem):
        pltpu.make_async_copy(ref, ref, sem).wait()

    src_31 = src.at[pl.ds(0, (OWNERS - 1) * CELLS)]
    for n in (2, 3, 4, 5, 6, 10, 12):
        loads[n].wait()
    outer = (outer_ref[0], outer_ref[1])
    inner = (inner_ref[0], inner_ref[1])

    wait_all(mu_send.at[pl.ds(0, OWNERS - 1)], all_recv.at[1])
    own_mu.wait()
    mu_high, mu_low = [], []
    for half in range(2):
        high_rows, low_rows = [], []
        for mode in range(NH):
            block = jnp.concatenate(
                decode(
                    mu_recv[half, mode, 0:8, :],
                    jnp.bitwise_and(mu_recv[half, mode, 8:9, :], 255) - 200,
                    weight_cube,
                ),
                axis=0,
            )
            high, low = halves(block)
            high_rows.append(high)
            low_rows.append(low)
        mu_high.append(jnp.concatenate(high_rows, axis=0))
        mu_low.append(jnp.concatenate(low_rows, axis=0))
    mu_cells = (jnp.concatenate(mu_high, axis=1), jnp.concatenate(mu_low, axis=1))
    first = halves(product(outer, mu_cells))
    inner_t = (inner_t_ref[0], inner_t_ref[1])
    outer_t = (outer_t_ref[0], outer_t_ref[1])
    line, square = line_buf[...], square_buf[...]
    back = []
    for block in range(3):
        here = slice(block * 128, block * 128 + 128)
        values = product((first[0][here], first[1][here]), inner)
        u_buf[here, :] = values
        weighted = []
        for n in range(8):
            a = block * 8 + n
            u = values[n * CELLS : n * CELLS + CELLS]
            x = float(nodes[a])
            form = (square + x * (line + x * col[0])) * ratio_ref[a : a + 1, :]
            weighted.append(u + u * form)
        back.append(product(halves(jnp.concatenate(weighted, axis=0)), inner_t))
    adj = product(outer_t, halves(jnp.concatenate(back, axis=0)))
    for mode in range(NH):
        for half in range(2):
            dest = 2 * mode + half
            block = adj[mode * CELLS : mode * CELLS + CELLS, half * WIDTH : half * WIDTH + WIDTH]
            word, level = encode(block[0:8], block[8:16])
            back_send[dest, 0:8, :] = word
            back_send[dest, 8:9, :] = level

    def send_back(step, _):
        z = lax.div(step, 2)
        late = z - 8
        z = jnp.where(z < 8, z, jnp.where(z < 12, 15 - late, late + 4))
        dest = lax.rem(step, 2) * 16 + z

        @pl.when(dest != me)
        def _():
            pltpu.make_async_remote_copy(
                src_ref=back_send.at[dest],
                dst_ref=back_recv.at[me],
                send_sem=all_send.at[3],
                recv_sem=all_recv.at[3],
                device_id={"coef": dest},
                device_id_type=MESH,
            ).start()

        return 0

    lax.fori_loop(0, OWNERS, send_back, 0)
    own_back = pltpu.make_async_copy(back_send.at[me], back_recv.at[me], local_sem.at[8])
    own_back.start()

    total = None
    for half in range(2):
        for mode in range(NH):
            row = sum_value(lax.shift_right_arithmetic(mu_recv[half, mode, 8:9, :], 8))
            total = row if total is None else total + row
    courant_buf[...] = jnp.broadcast_to(total, (8, 128))
    turn = lax.rem(128 - lax.div(me, 8) * CELLS, 128)
    turned = pltpu.roll(courant_buf[...], turn, 1) * (-1.0 / math.sqrt(K))
    out_courant[...] = turned[0:1, 0:CELLS]

    wait_all(src_31, all_recv.at[0])
    source = jnp.concatenate(
        [src_recv[0].reshape(256, WIDTH), src_recv[1].reshape(256, WIDTH)], axis=1
    )
    es_buf[...] = product(halves(product(outer, (source,))), inner)
    sums = [None, None, None]
    for a in range(QP):
        here = slice(a * CELLS, a * CELLS + CELLS)
        y = u_buf[here, :] * es_buf[here, :] * ratio_ref[a : a + 1, :]
        x = float(nodes[a])
        for n, term in enumerate((y, x * y, (x * x) * y)):
            sums[n] = term if sums[n] is None else sums[n] + term
    strain_sum = None
    for n in range(3):
        part = lax.dot_general(
            moments_ref[n],
            sums[n],
            (((1,), (1,)), ((), ())),
            precision=lax.Precision.HIGHEST,
            preferred_element_type=f32,
        )
        strain_sum = part if strain_sum is None else strain_sum + part
    out_strain[...] = strain_sum[0:9, :]

    own_back.wait()
    wait_all(src_31, all_send.at[0])
    wait_all(mu_send.at[pl.ds(0, OWNERS - 1)], all_send.at[1])
    wait_all(back_send.at[pl.ds(0, OWNERS - 1)], all_send.at[3])
    wait_all(back_send.at[pl.ds(0, OWNERS - 1)], all_recv.at[3])


def finish(back, strain, courant, out_source, out_strain, out_courant, source, sem):
    stores = [
        pltpu.make_async_copy(strain, out_strain, sem.at[0]),
        pltpu.make_async_copy(courant, out_courant, sem.at[1]),
    ]
    for copy in stores:
        copy.start()
    for part in range(4):
        for n in range(part * 8, part * 8 + 8):
            low, high = decode(back[n, 0:8, :], back[n, 8:9, :], 1.0)
            source[n * CELLS : n * CELLS + 8, :] = low
            source[n * CELLS + 8 : n * CELLS + 16, :] = high
        here = pl.ds(part * 128, 128)
        stores.append(pltpu.make_async_copy(source.at[here], out_source.at[here], sem.at[2 + part]))
        stores[-1].start()
    for copy in stores:
        copy.wait()


def body(cotangent, transport_state, source_state, courant, upwind_codes, strain_rate):
    nodes, *constants = tables()
    rows = PLANES * CYZ
    hbm = pl.BlockSpec(memory_space=pltpu.HBM)
    vmem = pl.BlockSpec(memory_space=pltpu.VMEM)
    results = pl.pallas_call(
        functools.partial(kernel, nodes),
        out_shape=(
            jax.ShapeDtypeStruct((OWNERS, 9, WIDTH), jnp.int32),
            jax.ShapeDtypeStruct((9, CELLS), f32),
            jax.ShapeDtypeStruct((1, CELLS), f32),
        ),
        in_specs=[hbm] * 13,
        out_specs=[vmem] * 3,
        scratch_shapes=[
            pltpu.VMEM((PLANES, CYZ, WIDTH), f32),
            pltpu.VMEM((3 * PLANES, CYZ, WIDTH), bf16),
            pltpu.VMEM((3, PLANES, CYZ), f32),
            pltpu.VMEM((128, 128), f32),
            pltpu.VMEM((8, PLANES, 9, WIDTH), jnp.int32),
            pltpu.VMEM((2, 8, PLANES, 9, WIDTH), jnp.int32),
            pltpu.VMEM((2, NH, CELLS, WIDTH), bf16),
            pltpu.VMEM((OWNERS, 9, WIDTH), jnp.int32),
            pltpu.VMEM((2, NH, 9, WIDTH), jnp.int32),
            pltpu.VMEM((OWNERS, 9, WIDTH), jnp.int32),
            pltpu.VMEM((PLANES, CYZ), f32),
            pltpu.VMEM((PLANES, CYZ), jnp.int32),
            pltpu.VMEM((9, CELLS), f32),
            pltpu.VMEM((2, QP * CELLS, NH * CELLS), bf16),
            pltpu.VMEM((2, NH * NH, POINTS), bf16),
            pltpu.VMEM((2, POINTS, NH * NH), bf16),
            pltpu.VMEM((2, NH * CELLS, QP * CELLS), bf16),
            pltpu.VMEM((QP, POINTS), f32),
            pltpu.VMEM((8, POINTS), f32),
            pltpu.VMEM((3, 16, POINTS), f32),
            pltpu.VMEM((QP * CELLS, POINTS), f32),
            pltpu.VMEM((QP * CELLS, POINTS), f32),
            pltpu.VMEM((CELLS, POINTS), f32),
            pltpu.VMEM((CELLS, POINTS), f32),
            pltpu.VMEM((128, 128), f32),
            pltpu.VMEM((8, WIDTH), f32),
            pltpu.SemaphoreType.DMA((15,)),
            pltpu.SemaphoreType.DMA((2, 17)),
            pltpu.SemaphoreType.DMA((2, 17)),
            pltpu.SemaphoreType.DMA((4,)),
            pltpu.SemaphoreType.DMA((4,)),
            pltpu.SemaphoreType.REGULAR((3,)),
        ],
        compiler_params=pltpu.CompilerParams(
            collective_id=0, has_side_effects=True, vmem_limit_bytes=30 * 2**20
        ),
    )(
        *[
            pltpu.with_memory_space_constraint(array, pltpu.HBM)
            for array in (
                cotangent.reshape(PLANES, CYZ, WIDTH),
                transport_state.reshape(PLANES, CYZ, WIDTH),
                source_state,
                courant.reshape(PLANES, CYZ),
                upwind_codes.reshape(PLANES, CYZ),
                strain_rate,
                *[jnp.asarray(table) for table in constants],
            )
        ],
    )
    adj_source, adj_strain, adj_courant = pl.pallas_call(
        finish,
        out_shape=(
            jax.ShapeDtypeStruct((rows, WIDTH), f32),
            jax.ShapeDtypeStruct((9, CELLS), f32),
            jax.ShapeDtypeStruct((1, CELLS), f32),
        ),
        in_specs=[vmem] * 3,
        out_specs=[hbm] * 3,
        scratch_shapes=[
            pltpu.VMEM((rows, WIDTH), f32),
            pltpu.SemaphoreType.DMA((6,)),
        ],
        compiler_params=pltpu.CompilerParams(vmem_limit_bytes=8 * 2**20),
    )(*results)
    return adj_source, adj_strain, adj_courant.reshape(CELLS)


def solution(mesh):
    placed = (
        P("slab", "coef"),
        P("slab", "coef"),
        P("slab", "coef"),
        P("slab"),
        P("slab"),
        P(None, ("slab", "coef")),
    )
    return jax.shard_map(
        body,
        mesh=mesh,
        in_specs=placed,
        out_specs=(P("slab", "coef"), P(None, ("slab", "coef")), P(("slab", "coef"))),
        check_vma=False,
    )
```
